128 devices in a mesh: cuts: 4 (over y_lo, core), probe: 32 (over z, x, y_hi).
Axes of the slice: x: 4, y: 4 (y_hi: 2, y_lo: 2; y = y_hi * 2 + y_lo), z: 4, core: 2. Of those that a mesh axis runs over, the one named last changes fastest.
Arguments:
- probe_modes: bfloat16 [256, 2, 512, 512], P(('cuts', 'probe')), may hold values from -6 to 6
- probe_corners: int32 [256, 2], P(('cuts', 'probe')), may hold values from 0 to 2047, as said below
- atom_cells: int32 [262144, 2], P(('cuts', 'probe')), may hold values from 0 to 2047, as said below
- atom_bins: int32 [262144, 1], P(('cuts', 'probe')), may hold values from 0 to 3; in each aligned block of 2048 rows (0 to 2047, 2048 to 4095, ...) at most 1024 rows name the same one
- atom_species: int32 [262144], P(('cuts', 'probe')), may hold values from 0 to 3
- species_amp: float32 [4], replicated, may hold values from 0.5 to 3
- species_width: float32 [4], replicated, may hold values from 0.7 to 2
- fresnel: bfloat16 [2, 512, 512], replicated, as said below
Outputs:
- exit_wave: float32 [256, 2, 512, 512], P(('cuts', 'probe'))
The draws below stay inside these ranges and needn't reach their ends.
Inputs may be any that keep to these rules, and one draw needn't show every extreme that they name: `atom_cells`: the atoms held by the device at index p along probe lie in grid rows p * 64 to (p + 1) * 64 - 1. `atom_bins`: among the 2048 atoms of one device (aligned blocks) no depth slice holds more than 1024. `probe_corners`: the probes held by the device at index q along probe have their first window row in the row block before q, counted round: grid rows ((q - 1) mod 32) * 64 to that plus 64 - 1. `fresnel`: both planes are zero where row and column indices differ by more than 6.
All inputs are finite; a program needn't handle non-finite values.
Results may differ from the reference program's by a relative error of at most 0.015.
Values may be sent and summed in bfloat16 or wider, within the bound.
A program may use at most 256 MiB of HBM per device.

```python
import math
import jax
import jax.numpy as jnp
import numpy as np
from jax import lax

NG = 2048
W = 512
HB = 6
NSPEC = 4
NA_DEV = 2048
PB_DEV = 2
CAP = 1024
TR = 64
SLICES = 4
ATOMS = 262144
PROBES = 256
N_CUTS = 4
N_PROBE = 32


def draw_probe_corners(key, part):
    key = jax.random.fold_in(key, 23)
    row_key, col_key = jax.random.split(key)
    owner_index = jnp.arange(PROBES, dtype=jnp.int32) // PB_DEV
    block_index = owner_index % N_PROBE
    row_pos = (block_index * TR - TR + NG + jax.random.randint(row_key, (PROBES,), 0, TR, dtype=jnp.int32)) % NG
    col_pos = jax.random.randint(col_key, (PROBES,), 0, NG, dtype=jnp.int32)
    return jnp.stack([row_pos, col_pos], axis=1)


def draw_atom_cells(key, part):
    key = jax.random.fold_in(key, 11)
    row_key, col_key = jax.random.split(key)
    owner_index = jnp.arange(ATOMS, dtype=jnp.int32) // NA_DEV
    block_index = owner_index % N_PROBE
    row_pos = block_index * TR + jax.random.randint(row_key, (ATOMS,), 0, TR, dtype=jnp.int32)
    col_pos = jax.random.randint(col_key, (ATOMS,), 0, NG, dtype=jnp.int32)
    return jnp.stack([row_pos, col_pos], axis=1)


def draw_fresnel(key, part):
    key = jax.random.fold_in(key, 17)
    real_key, imag_key, diag_key = jax.random.split(key, 3)
    positions = jnp.arange(W, dtype=jnp.int32)
    distance = jnp.abs(positions[:, None] - positions[None, :])
    inside = (distance <= HB).astype(jnp.float32)
    on_diagonal = distance == 0
    off_real = 0.1 * jax.random.normal(real_key, (W, W), jnp.float32)
    off_imag = 0.1 * jax.random.normal(imag_key, (W, W), jnp.float32)
    diagonal = jax.random.uniform(diag_key, (W, W), jnp.float32, 0.85, 1.05)
    real_plane = jnp.where(on_diagonal, diagonal, inside * off_real)
    imag_plane = inside * off_imag
    return jnp.stack([real_plane, imag_plane]).astype(jnp.bfloat16)


def with_ends(drawn, stream_key, low, largest):
    place = [jax.random.randint(jax.random.fold_in(stream_key, axis), (), 0, length) for axis, length in enumerate(drawn.shape)]
    longest = drawn.shape.index(max(drawn.shape))
    next_to = place[:longest] + [(place[longest] + 1) % drawn.shape[longest]] + place[longest + 1:]
    return drawn.at[tuple(place)].set(low).at[tuple(next_to)].set(largest)


def block_scale(key, shape, shards, least, top_value):
    loudness, own = 1.0, jax.random.fold_in(key, 6)
    for dim, parts in shards:
        draws = jnp.exp(jax.random.uniform(jax.random.fold_in(own, dim), (parts,), jnp.float32, least / len(shards), top_value / len(shards)))
        loudness = loudness * jnp.repeat(draws, shape[dim] // parts).reshape([-1 if axis == dim else 1 for axis in range(len(shape))])
    return loudness


def assign_block(rng, own, number, rows, number_of, top, limit, skew):
    order = jax.random.permutation(rng, number_of)
    crowded, ordinary = shares(number_of, rows * top, limit, skew, True), shares(number_of, rows * top, limit, skew, False)
    places = jnp.arange(number_of)

    def named(sizes, rotation):
        used = int((sizes > 0).sum())
        fixed = max(1, used // 4)
        shifted = fixed + (places - fixed + rotation * (used - fixed)) % max(1, number_of - fixed)
        return jnp.zeros((number_of,), jnp.int32).at[order[jnp.where(places < fixed, places, shifted)]].set(jnp.asarray(sizes, jnp.int32))

    sizes = jnp.where(number % 4 == 0, named(crowded, number // 4), named(ordinary, number - number // 4 - 1))
    mixed = jax.random.permutation(jax.random.fold_in(own, 3), number_of)
    donor, receiver = mixed[0:number_of // 2 * 2:2], mixed[1:number_of // 2 * 2:2]
    margin = jnp.minimum(sizes[donor] - 1, limit - sizes[receiver]) // 2
    margin = jnp.where((donor == order[0]) | (receiver == order[0]) | (sizes[receiver] == 0), 0, jnp.maximum(margin, 0))
    shifted = jax.random.randint(jax.random.fold_in(own, 4), (number_of // 2,), 0, 1 << 20) % (margin + 1)
    sizes = sizes.at[donor].add(-shifted).at[receiver].add(shifted)
    items = jnp.searchsorted(jnp.cumsum(sizes), jnp.arange(rows * top), side="right").astype(jnp.int32)
    table = items.reshape(top, rows).T
    table = table[jax.random.permutation(jax.random.fold_in(own, 1), rows)]
    rotation = jax.random.randint(jax.random.fold_in(own, 2), (rows, 1), 0, top)
    return jnp.take_along_axis(table, (jnp.arange(top)[None, :] + rotation) % top, axis=1)


def shares(amount, total, most, lean, full):
    loads = [(1 << 20) // math.isqrt(grade ** lean) + 1 for grade in range(1, amount + 1)]
    largest = most if full else min(most, max(-(-total // amount), total * loads[0] // sum(loads)))
    least = 1 if total - largest >= amount - 1 else 0
    holding, rest = [largest] + [least] * (amount - 1), total - largest - least * (amount - 1)
    while rest > 0:
        candidates = [i for i in range(1, amount) if holding[i] < largest] or [i for i in range(1, amount) if holding[i] < most]
        mass, remaining = sum([loads[i] for i in candidates]), rest
        for i in candidates:
            extra = min(most - holding[i], max(1, remaining * loads[i] // mass), rest)
            holding[i] = holding[i] + extra
            rest = rest - extra
    return np.array(holding)


def noise(key, shape, scale, most, cuts=(), kind=jnp.bfloat16):
    values = scale * jax.random.normal(key, shape, jnp.float32)
    if cuts:
        values = values * block_scale(key, shape, cuts, -0.22, 0.18)
    return jnp.clip(values, -most, most).astype(kind)


def setup_inputs(seed: int = 0) -> dict:
    seeds = jax.random.split(jax.random.key(seed), 9)
    probe_modes = noise(seeds[0], (PROBES, 2, W, W), 1.0, 6.0, ((0, 128),))
    probe_corners = draw_probe_corners(jax.random.fold_in(seeds[8], 71), 0)
    atom_cells = draw_atom_cells(jax.random.fold_in(seeds[8], 71), 0)
    atom_bins_keys = jax.random.split(jax.random.fold_in(seeds[3], 1), ATOMS // NA_DEV)
    atom_bins_turns = jax.random.permutation(jax.random.fold_in(seeds[3], 3), ATOMS // NA_DEV)
    atom_bins = jax.vmap(lambda own, number: assign_block(jax.random.fold_in(seeds[3], 2), own, number, NA_DEV, SLICES, 1, CAP, 2))(atom_bins_keys, atom_bins_turns).reshape((ATOMS, 1))
    atom_species = with_ends(jax.random.randint(seeds[4], (ATOMS,), 0, NSPEC), jax.random.fold_in(seeds[4], 1), 0, NSPEC - 1).astype(jnp.int32)
    species_amp = jnp.clip(jnp.exp(jax.random.uniform(seeds[5], (NSPEC,), jnp.float32, math.log(0.5), math.log(3.0))), 0.5, 3.0)
    species_width = jnp.clip(jnp.exp(jax.random.uniform(seeds[6], (NSPEC,), jnp.float32, math.log(0.7), math.log(2.0))), 0.7, 2.0)
    fresnel = draw_fresnel(jax.random.fold_in(seeds[8], 71), 0)
    return dict(probe_modes=probe_modes, probe_corners=probe_corners, atom_cells=atom_cells, atom_bins=atom_bins, atom_species=atom_species, species_amp=species_amp, species_width=species_width, fresnel=fresnel)


interaction = 0.4


def lookup(species, table):
    onehot = (species[:, None] == jnp.arange(NSPEC, dtype=jnp.int32)[None, :]).astype(jnp.float32)
    return jnp.sum(onehot * table[None, :], axis=1)


def row_profiles(local_row, strength, spread):
    grid_rows = jnp.arange(TR, dtype=jnp.float32)
    offset = grid_rows[None, :] - local_row[:, None]
    return strength[:, None] * jnp.exp(-offset * offset / (2.0 * spread[:, None] * spread[:, None]))


def column_profiles(col_pos, spread):
    grid_cols = jnp.arange(NG, dtype=jnp.float32)
    offset = grid_cols[None, :] - col_pos[:, None]
    return jnp.exp(-offset * offset / (2.0 * spread[:, None] * spread[:, None]))


def build_potential(atom_cells, atom_bins, atom_species, species_amp, species_width):
    cells = atom_cells.reshape(N_CUTS, N_PROBE, NA_DEV, 2)
    bins = atom_bins.reshape(N_CUTS, N_PROBE, NA_DEV)
    kinds = atom_species.reshape(N_CUTS, N_PROBE, NA_DEV)

    def one_block(block_index):
        block_cells = jnp.take(cells, block_index, axis=1).reshape(-1, 2)
        block_bins = jnp.take(bins, block_index, axis=1).reshape(-1)
        block_kinds = jnp.take(kinds, block_index, axis=1).reshape(-1)
        local_row = (block_cells[:, 0] % TR).astype(jnp.float32)
        col_pos = block_cells[:, 1].astype(jnp.float32)
        strength = lookup(block_kinds, species_amp)
        spread = lookup(block_kinds, species_width)
        rows_part = row_profiles(local_row, strength, spread)
        chosen = (block_bins[:, None] == jnp.arange(SLICES, dtype=jnp.int32)[None, :]).astype(jnp.float32)
        left = (chosen[:, :, None] * rows_part[:, None, :]).reshape(-1, SLICES * TR).astype(jnp.bfloat16)
        right = column_profiles(col_pos, spread).astype(jnp.bfloat16)
        return jnp.dot(left.T, right, preferred_element_type=jnp.float32)

    blocks = lax.map(one_block, jnp.arange(N_PROBE, dtype=jnp.int32))
    whole = blocks.reshape(N_PROBE, SLICES, TR, NG).transpose(1, 0, 2, 3).reshape(SLICES, NG, NG)
    return whole.astype(jnp.bfloat16)


def propagate(wave_pair, corner, potential, fresnel):
    fresnel_wide = fresnel.astype(jnp.float32)
    for layer_index in range(SLICES):
        window = lax.dynamic_slice(potential[layer_index], (corner[0], corner[1]), (W, W)).astype(jnp.float32)
        cosine = jnp.cos(interaction * window)
        sine = jnp.sin(interaction * window)
        real_part = wave_pair[0] * cosine - wave_pair[1] * sine
        imag_part = wave_pair[0] * sine + wave_pair[1] * cosine
        passed = jnp.stack([real_part, imag_part]).astype(jnp.bfloat16)
        left = jnp.einsum('cij,djk->cdik', fresnel_wide, passed.astype(jnp.float32))
        half = jnp.stack([left[0, 0] - left[1, 1], left[0, 1] + left[1, 0]]).astype(jnp.bfloat16)
        right = jnp.einsum('dij,ckj->cdik', half.astype(jnp.float32), fresnel_wide)
        wave_pair = jnp.stack([right[0, 0] - right[1, 1], right[1, 0] + right[0, 1]])
    return wave_pair


def reference(probe_modes, probe_corners, atom_cells, atom_bins, atom_species, species_amp, species_width, fresnel):
    potential = build_potential(atom_cells, atom_bins, atom_species, species_amp, species_width)
    periodic = jnp.concatenate([potential, potential[:, :W, :]], axis=1)
    periodic = jnp.concatenate([periodic, periodic[:, :, :W]], axis=2)

    def one_probe(item):
        return propagate(item[0].astype(jnp.float32), item[1], periodic, fresnel)

    return lax.map(one_probe, (probe_modes, probe_corners))
```

```python
import functools

import jax
import jax.numpy as jnp
from jax import lax
from jax.experimental import pallas as pl
from jax.experimental.pallas import tpu as pltpu
from jax.sharding import PartitionSpec as P

NG = 2048
W = 512
TR = 64
NSPEC = 4
NA = 2048
SLICES = 4
CUTS = 4
PROBE = 32
PB = 2

HALO = 9
LISTS = HALO * CUTS
CH = 128
NCH = NA // CH
BUCKET = 16
FIELDS = 5
PACK = FIELDS * NCH + 16
REACH = 28
CT = 256
PASS = 4
MESH = pl.DeviceIdType.MESH
F32 = jnp.float32
BF16 = jnp.bfloat16

PHASE = 0.4 / 6.283185307179586
COS = (
    0.9999992107823225,
    -19.738980355764074,
    64.92865742103473,
    -85.27162153430963,
    58.79049212015824,
    -21.071105627660344,
)
SIN = (
    6.283184916495432,
    -41.34158923268884,
    81.59994332978887,
    -76.61447253130079,
    41.34288235475198,
    -12.471243535265868,
)


def nn(a, b):
    return lax.dot_general(a, b, (((1,), (0,)), ((), ())), preferred_element_type=F32)


def nt(a, b):
    return lax.dot_general(a, b, (((1,), (1,)), ((), ())), preferred_element_type=F32)


def iota(shape, dim):
    return lax.broadcasted_iota(jnp.int32, shape, dim)


def sort_kernel(cells_ref, bins_ref, species_ref, out_ref):
    before = (iota((CH, CH), 0) < iota((CH, CH), 1)).astype(F32).astype(BF16)
    below = (iota((CH, CH), 1) < iota((CH, CH), 0)).astype(F32).astype(BF16)
    ones = jnp.ones((CH, CH), BF16)
    buckets = iota((CH, CH), 0)
    hots = []
    prefixes = []
    running = jnp.zeros((CH, CH), F32)
    by_lane = jnp.zeros((8, CH), F32)
    for c in range(NCH):
        lanes = slice(c * CH, (c + 1) * CH)
        column = cells_ref[1:2, lanes]
        hot = (buckets == column // BUCKET).astype(F32)
        hot16 = hot.astype(BF16)
        prefixes.append(nn(hot16, before) + running)
        running = running + nn(hot16, ones)
        by_lane = by_lane + nt(ones[:8], hot16)
        hots.append(hot)
    high = jnp.floor(running * (1.0 / 64.0))
    low = running - 64.0 * high
    offset = 64.0 * nn(below, high.astype(BF16)) + nn(below, low.astype(BF16))
    lane_high = jnp.floor(by_lane * (1.0 / 64.0))
    lane_low = by_lane - 64.0 * lane_high
    lane_offset = 64.0 * nn(lane_high.astype(BF16), before) + nn(lane_low.astype(BF16), before)
    sorted_fields = jnp.zeros((FIELDS * NCH, CH), F32)
    for c in range(NCH):
        lanes = slice(c * CH, (c + 1) * CH)
        rank = jnp.sum(hots[c] * (prefixes[c] + offset), axis=0, keepdims=True).astype(jnp.int32)
        row = cells_ref[0:1, lanes] & (TR - 1)
        column = cells_ref[1:2, lanes]
        fields = (row, column // 64, column & 63, species_ref[0:1, lanes], bins_ref[0:1, lanes])
        chosen = (iota((NCH, CH), 0) == rank // CH).astype(F32)
        left = jnp.concatenate([chosen * f.astype(F32) for f in fields], axis=0).astype(BF16)
        right = (buckets == (rank & (CH - 1))).astype(F32).astype(BF16)
        sorted_fields = sorted_fields + nt(left, right)
    top = jnp.floor(lane_offset * (1.0 / 64.0))
    out_ref[0 : FIELDS * NCH, :] = sorted_fields.astype(BF16)
    out_ref[FIELDS * NCH : PACK, :] = jnp.concatenate([top, lane_offset - 64.0 * top], axis=0).astype(BF16)


def gather_kernel(own_ref, out_ref, local_sem, send_sems, recv_sems):
    g = lax.axis_index("cuts")
    q = lax.axis_index("probe")
    barrier = pltpu.get_barrier_semaphore()
    pairs = [(j, r) for j in range(HALO) for r in range(CUTS) if (j, r) != (1, 0)]

    def holder(j, r):
        return lax.rem(g + r, CUTS), lax.rem(q + j - 1 + PROBE, PROBE)

    def reader(j, r):
        return lax.rem(g + r, CUTS), lax.rem(q + 1 - j + PROBE, PROBE)

    for j, r in pairs:
        pl.semaphore_signal(barrier, inc=1, device_id=holder(j, r), device_id_type=MESH)
    local = pltpu.make_async_copy(own_ref, out_ref.at[CUTS + g], local_sem)
    local.start()
    pl.semaphore_wait(barrier, len(pairs))
    sends = []
    for n, (j, r) in enumerate(pairs):
        slot = CUTS * j + g
        copy = pltpu.make_async_remote_copy(
            src_ref=own_ref,
            dst_ref=out_ref.at[slot],
            send_sem=send_sems.at[n],
            recv_sem=recv_sems.at[slot],
            device_id=reader(j, r),
            device_id_type=MESH,
        )
        copy.start()
        sends.append(copy)
    local.wait()
    for n, (j, r) in enumerate(pairs):
        slot = CUTS * j + lax.rem(g + r, CUTS)
        pltpu.make_async_remote_copy(
            src_ref=own_ref,
            dst_ref=out_ref.at[slot],
            send_sem=send_sems.at[n],
            recv_sem=recv_sems.at[slot],
            device_id=reader(j, r),
            device_id_type=MESH,
        ).wait_recv()
    for copy in sends:
        copy.wait_send()


LB = 96
LK = 128
NLB = -(-W // LB)
TPAD = 16
RIGHT_SPANS = ((0, 256), (0, 384), (128, 512), (256, 512))


def compute_kernel(
    corners_ref,
    amp_ref,
    width_ref,
    lists_ref,
    modes_ref,
    fresnel_ref,
    out_ref,
    col_ref,
    fall_ref,
    row_ref,
    str_ref,
    bin_ref,
    off_vec,
    off_ref,
    left_ref,
    right_ref,
    acc_ref,
    pot_ref,
    trans_ref,
    half_ref,
    lw_ref,
    rw0,
    rw1,
    rw2,
    rw3,
    sem,
):
    rws = (rw0, rw1, rw2, rw3)

    def unpack_offsets(i, carry):
        base = FIELDS * NCH
        high = lists_ref[i, base : base + 16, :].astype(F32)
        off_vec[pl.ds(i, 1), :] = (64.0 * high[0:1] + high[8:9]).astype(jnp.int32)
        return carry

    lax.fori_loop(0, LISTS, unpack_offsets, 0)
    copy = pltpu.make_async_copy(off_vec, off_ref, sem)
    copy.start()

    def unpack(i, carry):
        def part(f):
            return lists_ref[i, f * NCH : (f + 1) * NCH, :].astype(F32)

        species = part(3)
        amp = jnp.zeros((NCH, CH), F32)
        width = jnp.zeros((NCH, CH), F32)
        for s in range(NSPEC):
            amp = jnp.where(species == s, amp_ref[s], amp)
            width = jnp.where(species == s, width_ref[s], width)
        rows = pl.ds(pl.multiple_of(i * NCH, NCH), NCH)
        row_ref[rows, :] = part(0)
        col_ref[rows, :] = 64.0 * part(1) + part(2)
        fall_ref[rows, :] = -0.7213475204444817 / (width * width)
        str_ref[rows, :] = amp
        bin_ref[rows, :] = part(4)
        return carry

    lax.fori_loop(0, LISTS, unpack, 0)

    for b in range(NLB):
        n = min(LB, W - b * LB)
        turn = (TPAD - b * LB) % W
        for plane in range(2):
            rows = fresnel_ref[plane, b * LB : b * LB + n, :].astype(F32)
            block = pltpu.roll(rows, turn, 1)[:, :LK]
            if plane == 0:
                lw_ref[b, 0:n, 0:LK] = block.astype(BF16)
                lw_ref[b, LB : LB + n, LK : 2 * LK] = block.astype(BF16)
            else:
                lw_ref[b, 0:n, LK : 2 * LK] = (-block).astype(BF16)
                lw_ref[b, LB : LB + n, 0:LK] = block.astype(BF16)
    for b, (lo, hi) in enumerate(RIGHT_SPANS):
        k = hi - lo
        real = fresnel_ref[0, b * 128 : (b + 1) * 128, lo:hi]
        imag = fresnel_ref[1, b * 128 : (b + 1) * 128, lo:hi]
        rws[b][0:128, 0:k] = real
        rws[b][0:128, k : 2 * k] = -imag
        rws[b][128:256, 0:k] = imag
        rws[b][128:256, k : 2 * k] = real
    trans_ref[...] = jnp.zeros_like(trans_ref)
    copy.wait()

    tiles = W // CT

    def window_tile(n, carry):
        t = lax.rem(n, tiles)
        j = lax.rem(n // tiles, HALO)
        w = n // (tiles * HALO)
        shift = corners_ref[w, 0] & (TR - 1)
        first = (corners_ref[w, 1] + t * CT) & (NG - 1)
        rows = ((iota((TR, 1), 0) + shift) & (TR - 1)).astype(F32)
        columns = ((iota((CT, 1), 0) + first) & (NG - 1)).astype(F32)
        last = first + CT - 1 + REACH
        wraps = first + CT - 1 >= NG
        end_bucket = jnp.where(wraps, last - NG, jnp.minimum(last, NG - 1)) // BUCKET + 1
        start_bucket = jnp.maximum(first - REACH, 0) // BUCKET
        starts = []
        passes = jnp.int32(1)
        for l in range(CUTS):
            i = CUTS * j + l
            start = off_ref[i, start_bucket] // CH
            end = jnp.where(end_bucket >= NG // BUCKET, NA, off_ref[i, jnp.minimum(end_bucket, NG // BUCKET - 1)])
            end = jnp.where(wraps, end + NA, end)
            chunks = jnp.minimum((end + CH - 1) // CH - start, NCH)
            passes = jnp.maximum(passes, (chunks + PASS - 1) // PASS)
            starts.append(start)

        def one_pass(p, carry):
            total = None
            for l in range(CUTS):
                for m in range(PASS):
                    chunk = (starts[l] + p * PASS + m) & (NCH - 1)
                    at = pl.ds((CUTS * j + l) * NCH + chunk, 1)
                    lanes = slice(m * CH, (m + 1) * CH)
                    fall = fall_ref[at, :]
                    far = columns - col_ref[at, :]
                    right_ref[l, :, lanes] = jnp.exp2(far * far * fall).astype(BF16)
                    far = rows - row_ref[at, :]
                    profile = str_ref[at, :] * jnp.exp2(far * far * fall)
                    bins = bin_ref[at, :]
                    for k in range(SLICES):
                        left_ref[l, k * TR : (k + 1) * TR, lanes] = jnp.where(bins == k, profile, 0.0).astype(BF16)
                part = nt(left_ref[l], right_ref[l])
                total = part if total is None else total + part

            @pl.when(p == 0)
            def _():
                acc_ref[...] = total

            @pl.when(p > 0)
            def _():
                acc_ref[...] += total

            return carry

        lax.fori_loop(0, passes, one_pass, 0)
        for k in range(SLICES):
            for tt in range(tiles):

                @pl.when(t == tt)
                def _():
                    pot_ref[w, j, k, :, tt * CT : (tt + 1) * CT] = acc_ref[k * TR : (k + 1) * TR, :].astype(BF16)

        return carry

    lax.fori_loop(0, PB * HALO * tiles, window_tile, 0)

    for w in range(PB):
        out_ref[w] = modes_ref[w].astype(F32)
        shift = corners_ref[w, 0] & (TR - 1)
        upper = iota((TR, W), 0) + shift < TR

        def one_slice(k, carry):
            def transmit(i, carry):
                rows = pl.ds(pl.multiple_of(i * TR, TR), TR)
                window = jnp.where(upper, pot_ref[w, i, k].astype(F32), pot_ref[w, i + 1, k].astype(F32))
                turns = window * PHASE
                turns = turns - jnp.round(turns)
                square = turns * turns
                cosine = jnp.full_like(square, COS[-1])
                sine = jnp.full_like(square, SIN[-1])
                for a, b in zip(COS[-2::-1], SIN[-2::-1]):
                    cosine = cosine * square + a
                    sine = sine * square + b
                sine = sine * turns
                real = out_ref[w, 0, rows, :]
                imag = out_ref[w, 1, rows, :]
                into = pl.ds(pl.multiple_of(i * TR + TPAD, TPAD), TR)
                trans_ref[0, into, :] = (real * cosine - imag * sine).astype(BF16)
                trans_ref[1, into, :] = (real * sine + imag * cosine).astype(BF16)
                return carry

            lax.fori_loop(0, W // TR, transmit, 0)
            for b in range(NLB):
                n = min(LB, W - b * LB)
                rows = slice(b * LB, b * LB + LK)
                both = jnp.concatenate([trans_ref[0, rows, :], trans_ref[1, rows, :]], axis=0)
                product = nn(lw_ref[b], both).astype(BF16)
                half_ref[0, b * LB : b * LB + n, :] = product[0:n]
                half_ref[1, b * LB : b * LB + n, :] = product[LB : LB + n]
            for b, (lo, hi) in enumerate(RIGHT_SPANS):
                both = jnp.concatenate([half_ref[0, :, lo:hi], half_ref[1, :, lo:hi]], axis=1)
                product = nt(both, rws[b][...])
                out_ref[w, 0, :, b * 128 : (b + 1) * 128] = product[:, :128]
                out_ref[w, 1, :, b * 128 : (b + 1) * 128] = product[:, 128:]
            return carry

        lax.fori_loop(0, SLICES, one_slice, 0)


def compute(corners, amp, width, lists, modes, fresnel):
    smem = pl.BlockSpec(memory_space=pltpu.SMEM)
    vmem = pl.BlockSpec(memory_space=pltpu.VMEM)
    field = pltpu.VMEM((LISTS * NCH, CH), F32)
    return pl.pallas_call(
        compute_kernel,
        out_shape=jax.ShapeDtypeStruct((PB, 2, W, W), F32),
        in_specs=[smem, smem, smem, vmem, vmem, vmem],
        out_specs=vmem,
        scratch_shapes=[
            field,
            field,
            field,
            field,
            field,
            pltpu.VMEM((LISTS, CH), jnp.int32),
            pltpu.SMEM((LISTS, CH), jnp.int32),
            pltpu.VMEM((CUTS, SLICES * TR, PASS * CH), BF16),
            pltpu.VMEM((CUTS, CT, PASS * CH), BF16),
            pltpu.VMEM((SLICES * TR, CT), F32),
            pltpu.VMEM((PB, HALO, SLICES, TR, W), BF16),
            pltpu.VMEM((2, TPAD + W + 80, W), BF16),
            pltpu.VMEM((2, W, W), BF16),
            pltpu.VMEM((NLB, 2 * LB, 2 * LK), BF16),
        ]
        + [pltpu.VMEM((256, 2 * (hi - lo)), BF16) for lo, hi in RIGHT_SPANS]
        + [pltpu.SemaphoreType.DMA],
        compiler_params=pltpu.CompilerParams(vmem_limit_bytes=48 * 1024 * 1024),
        name="windows_and_slices",
    )(corners, amp, width, lists, modes, fresnel)


def sort_atoms(cells, bins, species):
    vmem = pl.BlockSpec(memory_space=pltpu.VMEM)
    return pl.pallas_call(
        sort_kernel,
        out_shape=jax.ShapeDtypeStruct((PACK, CH), BF16),
        in_specs=[vmem, vmem, vmem],
        out_specs=vmem,
        name="sort_atoms",
    )(cells, bins, species)


def gather_lists(own):
    return pl.pallas_call(
        gather_kernel,
        out_shape=jax.ShapeDtypeStruct((LISTS, PACK, CH), BF16),
        in_specs=[pl.BlockSpec(memory_space=pltpu.VMEM)],
        out_specs=pl.BlockSpec(memory_space=pl.ANY),
        scratch_shapes=[
            pltpu.SemaphoreType.DMA,
            pltpu.SemaphoreType.DMA((LISTS,)),
            pltpu.SemaphoreType.DMA((LISTS,)),
        ],
        compiler_params=pltpu.CompilerParams(collective_id=0, has_side_effects=True),
        name="gather_lists",
    )(own)


def body(
    probe_modes,
    probe_corners,
    atom_cells,
    atom_bins,
    atom_species,
    species_amp,
    species_width,
    fresnel,
):
    own = sort_atoms(atom_cells.T, atom_bins.T, atom_species.reshape(1, -1))
    lists = gather_lists(own)
    return compute(probe_corners, species_amp, species_width, lists, probe_modes, fresnel)


def solution(mesh):
    return jax.shard_map(
        body,
        mesh=mesh,
        in_specs=(
            P(("cuts", "probe"), None, None, None),
            P(("cuts", "probe"), None),
            P(("cuts", "probe"), None),
            P(("cuts", "probe"), None),
            P(("cuts", "probe")),
            P(),
            P(),
            P(),
        ),
        out_specs=P(("cuts", "probe"), None, None, None),
        check_vma=False,
    )
```

```python
import functools

import jax
import jax.numpy as jnp
from jax import lax
from jax.experimental import pallas as pl
from jax.experimental.pallas import tpu as pltpu
from jax.sharding import PartitionSpec as P

NG = 2048
W = 512
TR = 64
NSPEC = 4
NA = 2048
SLICES = 4
CUTS = 4
PROBE = 32
PB = 2

HALO = 9
LISTS = HALO * CUTS
CH = 128
NCH = NA // CH
BUCKET = 16
FIELDS = 5
PACK = FIELDS * NCH + 16
REACH = 28
CT = 256
GAP = 32
CLIP = 224.0
PASS = 4
MESH = pl.DeviceIdType.MESH
F32 = jnp.float32
BF16 = jnp.bfloat16

PHASE = 0.4 / 6.283185307179586
COS = (
    0.9999992107823225,
    -19.738980355764074,
    64.92865742103473,
    -85.27162153430963,
    58.79049212015824,
    -21.071105627660344,
)
SIN = (
    6.283184916495432,
    -41.34158923268884,
    81.59994332978887,
    -76.61447253130079,
    41.34288235475198,
    -12.471243535265868,
)


def nn(a, b):
    return lax.dot_general(a, b, (((1,), (0,)), ((), ())), preferred_element_type=F32)


def nt(a, b):
    return lax.dot_general(a, b, (((1,), (1,)), ((), ())), preferred_element_type=F32)


def iota(shape, dim):
    return lax.broadcasted_iota(jnp.int32, shape, dim)


def sort_kernel(cells_ref, bins_ref, species_ref, out_ref):
    before = (iota((CH, CH), 0) < iota((CH, CH), 1)).astype(F32).astype(BF16)
    below = (iota((CH, CH), 1) < iota((CH, CH), 0)).astype(F32).astype(BF16)
    ones = jnp.ones((CH, CH), BF16)
    buckets = iota((CH, CH), 0)
    hots = []
    prefixes = []
    running = jnp.zeros((CH, CH), F32)
    by_lane = jnp.zeros((8, CH), F32)
    for c in range(NCH):
        lanes = slice(c * CH, (c + 1) * CH)
        column = cells_ref[1:2, lanes]
        hot = (buckets == column // BUCKET).astype(F32)
        hot16 = hot.astype(BF16)
        prefixes.append(nn(hot16, before) + running)
        running = running + nn(hot16, ones)
        by_lane = by_lane + nt(ones[:8], hot16)
        hots.append(hot)
    high = jnp.floor(running * (1.0 / 64.0))
    low = running - 64.0 * high
    offset = 64.0 * nn(below, high.astype(BF16)) + nn(below, low.astype(BF16))
    lane_high = jnp.floor(by_lane * (1.0 / 64.0))
    lane_low = by_lane - 64.0 * lane_high
    lane_offset = 64.0 * nn(lane_high.astype(BF16), before) + nn(lane_low.astype(BF16), before)
    sorted_fields = jnp.zeros((FIELDS * NCH, CH), F32)
    for c in range(NCH):
        lanes = slice(c * CH, (c + 1) * CH)
        rank = jnp.sum(hots[c] * (prefixes[c] + offset), axis=0, keepdims=True).astype(jnp.int32)
        row = cells_ref[0:1, lanes] & (TR - 1)
        column = cells_ref[1:2, lanes]
        fields = (row, column // 64, column & 63, species_ref[0:1, lanes], bins_ref[0:1, lanes])
        chosen = (iota((NCH, CH), 0) == rank // CH).astype(F32)
        left = jnp.concatenate([chosen * f.astype(F32) for f in fields], axis=0).astype(BF16)
        right = (buckets == (rank & (CH - 1))).astype(F32).astype(BF16)
        sorted_fields = sorted_fields + nt(left, right)
    top = jnp.floor(lane_offset * (1.0 / 64.0))
    out_ref[0 : FIELDS * NCH, :] = sorted_fields.astype(BF16)
    out_ref[FIELDS * NCH : PACK, :] = jnp.concatenate([top, lane_offset - 64.0 * top], axis=0).astype(BF16)


def gather_kernel(own_ref, out_ref, local_sem, send_sems, recv_sems):
    g = lax.axis_index("cuts")
    q = lax.axis_index("probe")
    barrier = pltpu.get_barrier_semaphore()
    pairs = [(j, r) for j in range(HALO) for r in range(CUTS) if (j, r) != (1, 0)]

    def holder(j, r):
        return lax.rem(g + r, CUTS), lax.rem(q + j - 1 + PROBE, PROBE)

    def reader(j, r):
        return lax.rem(g + r, CUTS), lax.rem(q + 1 - j + PROBE, PROBE)

    for j, r in pairs:
        pl.semaphore_signal(barrier, inc=1, device_id=holder(j, r), device_id_type=MESH)
    local = pltpu.make_async_copy(own_ref, out_ref.at[CUTS + g], local_sem)
    local.start()
    pl.semaphore_wait(barrier, len(pairs))
    sends = []
    for n, (j, r) in enumerate(pairs):
        slot = CUTS * j + g
        copy = pltpu.make_async_remote_copy(
            src_ref=own_ref,
            dst_ref=out_ref.at[slot],
            send_sem=send_sems.at[n],
            recv_sem=recv_sems.at[slot],
            device_id=reader(j, r),
            device_id_type=MESH,
        )
        copy.start()
        sends.append(copy)
    local.wait()
    for n, (j, r) in enumerate(pairs):
        slot = CUTS * j + lax.rem(g + r, CUTS)
        pltpu.make_async_remote_copy(
            src_ref=own_ref,
            dst_ref=out_ref.at[slot],
            send_sem=send_sems.at[n],
            recv_sem=recv_sems.at[slot],
            device_id=reader(j, r),
            device_id_type=MESH,
        ).wait_recv()
    for copy in sends:
        copy.wait_send()


GR = 32
LB = 96
LK = 128
NLB = -(-W // LB)
TPAD = 16
RIGHT_SPANS = ((0, 256), (0, 384), (128, 512), (256, 512))


def compute_kernel(
    corners_hbm,
    amp_hbm,
    width_hbm,
    lists_hbm,
    modes_hbm,
    fresnel_hbm,
    out_hbm,
    corners_ref,
    amp_ref,
    width_ref,
    lists_ref,
    modes_ref,
    fresnel_ref,
    out_ref,
    col_ref,
    fall_ref,
    row_ref,
    str_ref,
    bin_ref,
    off_vec,
    off_ref,
    left0,
    right0,
    left1,
    right1,
    acc_ref,
    pot_ref,
    trans0,
    trans1,
    half0,
    half1,
    lw_ref,
    rw0,
    rw1,
    rw2,
    rw3,
    sem,
    in_sems,
    out_sems,
):
    rws = (rw0, rw1, rw2, rw3)
    sources = (lists_hbm, corners_hbm, amp_hbm, width_hbm, fresnel_hbm, modes_hbm)
    targets = (lists_ref, corners_ref, amp_ref, width_ref, fresnel_ref, modes_ref)
    fetches = [pltpu.make_async_copy(a, b, in_sems.at[n]) for n, (a, b) in enumerate(zip(sources, targets))]
    for fetch in fetches:
        fetch.start()
    for fetch in fetches[:4]:
        fetch.wait()

    def unpack_offsets(i, carry):
        base = FIELDS * NCH
        high = lists_ref[i, base : base + 16, :].astype(F32)
        off_vec[pl.ds(i, 1), :] = (64.0 * high[0:1] + high[8:9]).astype(jnp.int32)
        return carry

    lax.fori_loop(0, LISTS, unpack_offsets, 0)
    copy = pltpu.make_async_copy(off_vec, off_ref, sem)
    copy.start()

    def unpack(i, carry):
        def part(f):
            return lists_ref[i, f * NCH : (f + 1) * NCH, :].astype(F32)

        species = part(3)
        amp = jnp.zeros((NCH, CH), F32)
        width = jnp.zeros((NCH, CH), F32)
        for s in range(NSPEC):
            amp = jnp.where(species == s, amp_ref[s], amp)
            width = jnp.where(species == s, width_ref[s], width)
        rows = pl.ds(pl.multiple_of(i * NCH, NCH), NCH)
        row_ref[rows, :] = part(0)
        col_ref[rows, :] = 64.0 * part(1) + part(2)
        fall_ref[rows, :] = -0.7213475204444817 / (width * width)
        str_ref[rows, :] = amp
        bin_ref[rows, :] = part(4)
        return carry

    lax.fori_loop(0, LISTS, unpack, 0)

    copy.wait()
    tiles = W // CT

    def which(n):
        w = jnp.where(n >= HALO, 1, 0)
        return w, n - HALO * w

    def place(w, t):
        first = (corners_ref[w, 1] + t * CT) & (NG - 1)
        return first, first + CT > NG

    def chunk_range(w, j, t):
        first, wraps = place(w, t)
        last = first + CT - 1 + REACH
        end_bucket = jnp.where(wraps, last - NG, jnp.minimum(last, NG - 1)) // BUCKET + 1
        start_bucket = jnp.maximum(first - REACH, 0) // BUCKET
        starts = []
        passes = jnp.int32(1)
        for l in range(CUTS):
            i = CUTS * j + l
            start = off_ref[i, start_bucket] // CH
            end = jnp.where(end_bucket >= NG // BUCKET, NA, off_ref[i, jnp.minimum(end_bucket, NG // BUCKET - 1)])
            end = jnp.where(wraps, end + NA, end)
            chunks = jnp.minimum((end + CH - 1) // CH - start, NCH)
            passes = jnp.maximum(passes, (chunks + PASS - 1) // PASS)
            starts.append(start)
        return starts, passes

    def fill(w, j, t, starts, p, left, right):
        first, wraps = place(w, t)
        shift = corners_ref[w, 0] & (TR - 1)
        rows = ((iota((TR, 1), 0) + shift) & (TR - 1)).astype(F32)
        step = iota((CT, 1), 0)
        gap = jnp.where(step >= NG - first, GAP, 0)
        columns = jnp.broadcast_to((step - CT // 2 + gap).astype(F32), (CT, CH)).astype(BF16)
        origin = (first + CT // 2).astype(F32)
        beyond = jnp.where(wraps, NG // 2, -1).astype(F32)
        for l in range(CUTS):
            for m in range(PASS):
                chunk = (starts[l] + p * PASS + m) & (NCH - 1)
                at = pl.ds((CUTS * j + l) * NCH + chunk, 1)
                c = l * PASS + m
                fall = fall_ref[at, :]
                column = col_ref[at, :]
                column = column - origin + jnp.where(column < beyond, float(NG + GAP), 0.0)
                column = jnp.clip(column, -CLIP, CLIP)
                column16 = jnp.broadcast_to(column, (16, CH)).astype(BF16)
                fall16 = jnp.broadcast_to(fall, (16, CH)).astype(BF16)
                for s in range(CT // 16):
                    far = columns[16 * s : 16 * s + 16] - column16
                    right[c, 16 * s : 16 * s + 16, :] = jnp.exp2(far * far * fall16)
                far = rows - row_ref[at, :]
                profile = (str_ref[at, :] * jnp.exp2(far * far * fall)).astype(BF16)
                bins = jnp.broadcast_to(bin_ref[at, :], (16, CH))
                for k in range(SLICES):
                    mask = (bins == k).astype(F32).astype(BF16)
                    for s in range(TR // 16):
                        left[c, k * TR + 16 * s : k * TR + 16 * s + 16, :] = profile[16 * s : 16 * s + 16] * mask

    def product(left, right):
        wide = [jnp.concatenate([ref[c] for c in range(CUTS * PASS)], axis=1) for ref in (left, right)]
        return nt(*wide)

    def store(w, j, t, value):
        for k in range(SLICES):
            pot_ref[w, j, k, :, t * CT : (t + 1) * CT] = value[k * TR : (k + 1) * TR].astype(BF16)

    def window_blocks(n, most):
        w, j = which(n)
        values = [product(left, right) for left, right in buffers]
        for t, (left, right) in enumerate(buffers):
            starts, passes = chunk_range(w, j, t)
            most = jnp.maximum(most, passes)
            fill(w, j, t, starts, 0, left, right)
        before = which(jnp.maximum(n - 1, 0))
        for t, value in enumerate(values):
            store(*before, t, value)
        return most

    buffers = ((left0, right0), (left1, right1))
    most = lax.fori_loop(0, PB * HALO, window_blocks, jnp.int32(1))
    for t, (left, right) in enumerate(buffers):
        store(PB - 1, HALO - 1, t, product(left, right))

    def crowded(n, carry):
        w, j = which(n)
        for t in range(tiles):
            starts, passes = chunk_range(w, j, t)

            @pl.when(passes > 1)
            def _():
                acc_ref[...] = jnp.zeros_like(acc_ref)

                def one_pass(p, carry):
                    fill(w, j, t, starts, p, left0, right0)
                    acc_ref[...] += product(left0, right0)
                    return carry

                lax.fori_loop(0, passes, one_pass, 0)
                store(w, j, t, acc_ref[...])

        return carry

    lax.fori_loop(0, jnp.where(most > 1, PB * HALO, 0), crowded, 0)

    for fetch in fetches[4:]:
        fetch.wait()
    for b in range(NLB):
        n = min(LB, W - b * LB)
        turn = (TPAD - b * LB) % W
        for plane in range(2):
            rows = fresnel_ref[plane, b * LB : b * LB + n, :].astype(F32)
            block = pltpu.roll(rows, turn, 1)[:, :LK]
            if plane == 0:
                lw_ref[b, 0:n, 0:LK] = block.astype(BF16)
                lw_ref[b, LB : LB + n, LK : 2 * LK] = block.astype(BF16)
            else:
                lw_ref[b, 0:n, LK : 2 * LK] = (-block).astype(BF16)
                lw_ref[b, LB : LB + n, 0:LK] = block.astype(BF16)
    for b, (lo, hi) in enumerate(RIGHT_SPANS):
        k = hi - lo
        real = fresnel_ref[0, b * 128 : (b + 1) * 128, lo:hi]
        imag = fresnel_ref[1, b * 128 : (b + 1) * 128, lo:hi]
        rws[b][0:128, 0:k] = real
        rws[b][0:128, k : 2 * k] = -imag
        rws[b][128:256, 0:k] = imag
        rws[b][128:256, k : 2 * k] = real
    trans0[...] = jnp.zeros_like(trans0)
    trans1[...] = jnp.zeros_like(trans1)

    for w in range(PB):
        out_ref[w] = modes_ref[w].astype(F32)

    def transmit(w, k, trans):
        shift = corners_ref[w, 0] & (TR - 1)
        upper = iota((GR, W), 0) + shift

        def group(i):
            block, part = i * GR // TR, i * GR % TR
            rows = slice(i * GR, (i + 1) * GR)
            inner = slice(part, part + GR)
            window = jnp.where(
                upper + part < TR,
                pot_ref[w, block, k, inner, :].astype(F32),
                pot_ref[w, block + 1, k, inner, :].astype(F32),
            )
            turns = window * PHASE
            turns = turns - jnp.round(turns)
            square = turns * turns
            cosine = jnp.full_like(square, COS[-1])
            sine = jnp.full_like(square, SIN[-1])
            for a, b in zip(COS[-2::-1], SIN[-2::-1]):
                cosine = cosine * square + a
                sine = sine * square + b
            sine = sine * turns
            real = out_ref[w, 0, rows, :]
            imag = out_ref[w, 1, rows, :]
            into = slice(i * GR + TPAD, (i + 1) * GR + TPAD)
            trans[0, into, :] = (real * cosine - imag * sine).astype(BF16)
            trans[1, into, :] = (real * sine + imag * cosine).astype(BF16)

        return [functools.partial(group, i) for i in range(W // GR)]

    def propagate(w, trans, half):
        def left(b):
            n = min(LB, W - b * LB)
            rows = slice(b * LB, b * LB + LK)
            both = jnp.concatenate([trans[0, rows, :], trans[1, rows, :]], axis=0)
            product = nn(lw_ref[b], both).astype(BF16)
            half[0, b * LB : b * LB + n, :] = product[0:n]
            half[1, b * LB : b * LB + n, :] = product[LB : LB + n]

        def right(b):
            lo, hi = RIGHT_SPANS[b]
            both = jnp.concatenate([half[0, :, lo:hi], half[1, :, lo:hi]], axis=1)
            product = nt(both, rws[b][...])
            out_ref[w, 0, :, b * 128 : (b + 1) * 128] = product[:, :128]
            out_ref[w, 1, :, b * 128 : (b + 1) * 128] = product[:, 128:]

        pieces = [(1.0, functools.partial(left, b)) for b in range(NLB)]
        return pieces + [(3.3, functools.partial(right, b)) for b in range(4)]

    def together(pieces, groups):
        total = sum(cost for cost, _ in pieces)
        done, at = 0, 0.0
        for cost, piece in pieces:
            piece()
            at += cost
            until = round(at / total * len(groups))
            for group in groups[done:until]:
                group()
            done = until

    def send(w):
        return pltpu.make_async_copy(out_ref.at[w], out_hbm.at[w], out_sems.at[w])

    for group in transmit(0, 0, trans0):
        group()

    def one_slice(k, carry):
        @pl.when(corners_ref[0, 0] >= 0)
        def _():
            together(propagate(0, trans0, half0), transmit(1, k, trans1))

        @pl.when(corners_ref[0, 0] >= 0)
        def _():
            together(propagate(1, trans1, half1), transmit(0, k + 1, trans0))

        return carry

    lax.fori_loop(0, SLICES - 1, one_slice, 0)
    together(propagate(0, trans0, half0), transmit(1, SLICES - 1, trans1))
    send(0).start()
    together(propagate(1, trans1, half1), [])
    send(1).start()
    for w in range(PB):
        send(w).wait()


def compute(corners, amp, width, lists, modes, fresnel):
    hbm = pl.BlockSpec(memory_space=pltpu.HBM)
    field = pltpu.VMEM((LISTS * NCH, CH), F32)
    return pl.pallas_call(
        compute_kernel,
        out_shape=jax.ShapeDtypeStruct((PB, 2, W, W), F32),
        in_specs=[hbm] * 6,
        out_specs=hbm,
        scratch_shapes=[
            pltpu.SMEM((PB, 2), jnp.int32),
            pltpu.SMEM((NSPEC,), F32),
            pltpu.SMEM((NSPEC,), F32),
            pltpu.VMEM((LISTS, PACK, CH), BF16),
            pltpu.VMEM((PB, 2, W, W), BF16),
            pltpu.VMEM((2, W, W), BF16),
            pltpu.VMEM((PB, 2, W, W), F32),
            field,
            field,
            field,
            field,
            field,
            pltpu.VMEM((LISTS, CH), jnp.int32),
            pltpu.SMEM((LISTS, CH), jnp.int32),
            pltpu.VMEM((CUTS * PASS, SLICES * TR, CH), BF16),
            pltpu.VMEM((CUTS * PASS, CT, CH), BF16),
            pltpu.VMEM((CUTS * PASS, SLICES * TR, CH), BF16),
            pltpu.VMEM((CUTS * PASS, CT, CH), BF16),
            pltpu.VMEM((SLICES * TR, CT), F32),
            pltpu.VMEM((PB, HALO, SLICES, TR, W), BF16),
            pltpu.VMEM((2, TPAD + W + 80, W), BF16),
            pltpu.VMEM((2, TPAD + W + 80, W), BF16),
            pltpu.VMEM((2, W, W), BF16),
            pltpu.VMEM((2, W, W), BF16),
            pltpu.VMEM((NLB, 2 * LB, 2 * LK), BF16),
        ]
        + [pltpu.VMEM((256, 2 * (hi - lo)), BF16) for lo, hi in RIGHT_SPANS]
        + [pltpu.SemaphoreType.DMA, pltpu.SemaphoreType.DMA((6,)), pltpu.SemaphoreType.DMA((PB,))],
        compiler_params=pltpu.CompilerParams(vmem_limit_bytes=60 * 1024 * 1024),
        name="windows_and_slices",
    )(corners, amp, width, lists, modes, fresnel)


def sort_atoms(cells, bins, species):
    vmem = pl.BlockSpec(memory_space=pltpu.VMEM)
    return pl.pallas_call(
        sort_kernel,
        out_shape=jax.ShapeDtypeStruct((PACK, CH), BF16),
        in_specs=[vmem, vmem, vmem],
        out_specs=vmem,
        name="sort_atoms",
    )(cells, bins, species)


def gather_lists(own):
    return pl.pallas_call(
        gather_kernel,
        out_shape=jax.ShapeDtypeStruct((LISTS, PACK, CH), BF16),
        in_specs=[pl.BlockSpec(memory_space=pltpu.VMEM)],
        out_specs=pl.BlockSpec(memory_space=pl.ANY),
        scratch_shapes=[
            pltpu.SemaphoreType.DMA,
            pltpu.SemaphoreType.DMA((LISTS,)),
            pltpu.SemaphoreType.DMA((LISTS,)),
        ],
        compiler_params=pltpu.CompilerParams(collective_id=0, has_side_effects=True),
        name="gather_lists",
    )(own)


def body(
    probe_modes,
    probe_corners,
    atom_cells,
    atom_bins,
    atom_species,
    species_amp,
    species_width,
    fresnel,
):
    own = sort_atoms(atom_cells.T, atom_bins.T, atom_species.reshape(1, -1))
    lists = gather_lists(own)
    return compute(probe_corners, species_amp, species_width, lists, probe_modes, fresnel)


def solution(mesh):
    return jax.shard_map(
        body,
        mesh=mesh,
        in_specs=(
            P(("cuts", "probe"), None, None, None),
            P(("cuts", "probe"), None),
            P(("cuts", "probe"), None),
            P(("cuts", "probe"), None),
            P(("cuts", "probe")),
            P(),
            P(),
            P(),
        ),
        out_specs=P(("cuts", "probe"), None, None, None),
        check_vma=False,
    )
```

```python
import functools

import jax
import jax.numpy as jnp
from jax import lax
from jax.experimental import pallas as pl
from jax.experimental.pallas import tpu as pltpu
from jax.sharding import PartitionSpec as P

NG = 2048
W = 512
TR = 64
NSPEC = 4
NA = 2048
SLICES = 4
CUTS = 4
PROBE = 32
PB = 2

HALO = 9
LISTS = HALO * CUTS
CH = 128
NCH = NA // CH
BUCKET = 16
FIELDS = 5
PACK = FIELDS * NCH + 16
REACH = 13.7
CT = 256
GAP = 32
CLIP = 224.0
PASS = 4
MESH = pl.DeviceIdType.MESH
F32 = jnp.float32
BF16 = jnp.bfloat16

PHASE = 0.4 / 6.283185307179586
COS = (
    0.9999992107823225,
    -19.738980355764074,
    64.92865742103473,
    -85.27162153430963,
    58.79049212015824,
    -21.071105627660344,
)
SIN = (
    6.283184916495432,
    -41.34158923268884,
    81.59994332978887,
    -76.61447253130079,
    41.34288235475198,
    -12.471243535265868,
)


def nn(a, b):
    return lax.dot_general(a, b, (((1,), (0,)), ((), ())), preferred_element_type=F32)


def nt(a, b):
    return lax.dot_general(a, b, (((1,), (1,)), ((), ())), preferred_element_type=F32)


def iota(shape, dim):
    return lax.broadcasted_iota(jnp.int32, shape, dim)


def sort_into(cells_ref, bins_ref, species_ref, out_ref):
    before = (iota((CH, CH), 0) < iota((CH, CH), 1)).astype(F32).astype(BF16)
    below = (iota((CH, CH), 1) < iota((CH, CH), 0)).astype(F32).astype(BF16)
    ones = jnp.ones((CH, CH), BF16)
    buckets = iota((CH, CH), 0)
    hots = []
    prefixes = []
    running = jnp.zeros((CH, CH), F32)
    by_lane = jnp.zeros((8, CH), F32)
    for c in range(NCH):
        lanes = slice(c * CH, (c + 1) * CH)
        column = cells_ref[1:2, lanes]
        hot = (buckets == column // BUCKET).astype(F32)
        hot16 = hot.astype(BF16)
        prefixes.append(nn(hot16, before) + running)
        running = running + nn(hot16, ones)
        by_lane = by_lane + nt(ones[:8], hot16)
        hots.append(hot)
    high = jnp.floor(running * (1.0 / 64.0))
    low = running - 64.0 * high
    offset = 64.0 * nn(below, high.astype(BF16)) + nn(below, low.astype(BF16))
    lane_high = jnp.floor(by_lane * (1.0 / 64.0))
    lane_low = by_lane - 64.0 * lane_high
    lane_offset = 64.0 * nn(lane_high.astype(BF16), before) + nn(lane_low.astype(BF16), before)
    sorted_fields = jnp.zeros((FIELDS * NCH, CH), F32)
    for c in range(NCH):
        lanes = slice(c * CH, (c + 1) * CH)
        rank = jnp.sum(hots[c] * (prefixes[c] + offset), axis=0, keepdims=True).astype(jnp.int32)
        row = cells_ref[0:1, lanes] & (TR - 1)
        column = cells_ref[1:2, lanes]
        fields = (row, column // 64, column & 63, species_ref[0:1, lanes], bins_ref[0:1, lanes])
        chosen = (iota((NCH, CH), 0) == rank // CH).astype(F32)
        left = jnp.concatenate([chosen * f.astype(F32) for f in fields], axis=0).astype(BF16)
        right = (buckets == (rank & (CH - 1))).astype(F32).astype(BF16)
        sorted_fields = sorted_fields + nt(left, right)
    top = jnp.floor(lane_offset * (1.0 / 64.0))
    out_ref[0 : FIELDS * NCH, :] = sorted_fields.astype(BF16)
    out_ref[FIELDS * NCH : PACK, :] = jnp.concatenate([top, lane_offset - 64.0 * top], axis=0).astype(BF16)


def lists_kernel(cells_ref, bins_ref, species_ref, out_ref, own_ref, local_sem, send_sems, pass_sems, recv_sems):
    g = lax.axis_index("cuts")
    q = lax.axis_index("probe")
    core = lax.rem(g, 2)
    sibling = (g + 1 - 2 * core, q)
    barrier = pltpu.get_barrier_semaphore()
    pairs = [(j, r) for j in (1, 2, 0, 3, 4, 5, 6, 7, 8) for r in (0, 2) if (j, r) != (1, 0)]

    def holder(j, r):
        return lax.rem(g + r, CUTS), lax.rem(q + j - 1 + PROBE, PROBE)

    def reader(j, r):
        return lax.rem(g + r, CUTS), lax.rem(q + 1 - j + PROBE, PROBE)

    def remote(src, slot, send_sem, device):
        return pltpu.make_async_remote_copy(
            src_ref=src,
            dst_ref=out_ref.at[slot],
            send_sem=send_sem,
            recv_sem=recv_sems.at[slot],
            device_id=device,
            device_id_type=MESH,
        )

    pl.semaphore_signal(barrier, inc=1, device_id=sibling, device_id_type=MESH)
    for j, r in pairs:
        pl.semaphore_signal(barrier, inc=1, device_id=holder(j, r), device_id_type=MESH)
    sort_into(cells_ref, bins_ref, species_ref, own_ref)
    local = pltpu.make_async_copy(own_ref, out_ref.at[CUTS + g], local_sem)
    local.start()
    pl.semaphore_wait(barrier, len(pairs) + 1)
    sends = []
    for n, (j, r) in enumerate(pairs):
        sends.append(remote(own_ref, CUTS * j + g, send_sems.at[n], reader(j, r)))
    sends.append(remote(own_ref, CUTS + g, pass_sems.at[len(pairs)], sibling))
    for copy in sends:
        copy.start()
    for n, (j, r) in enumerate(pairs):
        slot = CUTS * j + lax.rem(g + r, CUTS)
        remote(own_ref, slot, send_sems.at[n], sibling).wait_recv()
        onward = remote(out_ref.at[slot], slot, pass_sems.at[n], sibling)
        onward.start()
        sends.append(onward)
    for j in range(HALO):
        for r in (1, 3):
            slot = CUTS * j + lax.rem(g + r, CUTS)
            remote(own_ref, slot, send_sems.at[0], sibling).wait_recv()
    for copy in sends:
        copy.wait_send()
    local.wait()


GR = 32
LB = 96
LK = 128
NLB = -(-W // LB)
TPAD = 16
RIGHT_SPANS = ((0, 256), (0, 384), (128, 512), (256, 512))


def compute_kernel(
    corners_hbm,
    amp_hbm,
    width_hbm,
    lists_hbm,
    modes_hbm,
    fresnel_hbm,
    out_hbm,
    corners_ref,
    amp_ref,
    width_ref,
    lists_ref,
    modes_ref,
    fresnel_ref,
    out_ref,
    col_ref,
    fall_ref,
    row_ref,
    str_ref,
    bin_ref,
    off_vec,
    off_ref,
    left0,
    right0,
    left1,
    right1,
    acc_ref,
    pot_ref,
    trans0,
    trans1,
    half0,
    half1,
    lw_ref,
    rw0,
    rw1,
    rw2,
    rw3,
    sem,
    busy_ref,
    in_sems,
    out_sems,
):
    rws = (rw0, rw1, rw2, rw3)
    sources = (lists_hbm, corners_hbm, amp_hbm, width_hbm, fresnel_hbm, modes_hbm)
    targets = (lists_ref, corners_ref, amp_ref, width_ref, fresnel_ref, modes_ref)
    fetches = [pltpu.make_async_copy(a, b, in_sems.at[n]) for n, (a, b) in enumerate(zip(sources, targets))]
    for fetch in fetches:
        fetch.start()
    for fetch in fetches[:4]:
        fetch.wait()

    def unpack_offsets(i, carry):
        base = FIELDS * NCH
        high = lists_ref[i, base : base + 16, :].astype(F32)
        off_vec[pl.ds(i, 1), :] = (64.0 * high[0:1] + high[8:9]).astype(jnp.int32)
        return carry

    lax.fori_loop(0, LISTS, unpack_offsets, 0)
    copy = pltpu.make_async_copy(off_vec, off_ref, sem)
    copy.start()

    def unpack(i, carry):
        def part(f):
            return lists_ref[i, f * NCH : (f + 1) * NCH, :].astype(F32)

        species = part(3)
        amp = jnp.zeros((NCH, CH), F32)
        width = jnp.zeros((NCH, CH), F32)
        for s in range(NSPEC):
            amp = jnp.where(species == s, amp_ref[s], amp)
            width = jnp.where(species == s, width_ref[s], width)
        rows = pl.ds(pl.multiple_of(i * NCH, NCH), NCH)
        row_ref[rows, :] = part(0)
        col_ref[rows, :] = 64.0 * part(1) + part(2)
        fall_ref[rows, :] = -0.7213475204444817 / (width * width)
        str_ref[rows, :] = amp
        bin_ref[rows, :] = part(4)
        return carry

    lax.fori_loop(0, LISTS, unpack, 0)

    copy.wait()
    tiles = W // CT

    widest = width_ref[0]
    for species in range(1, NSPEC):
        widest = jnp.maximum(widest, width_ref[species])
    reach = (widest * REACH).astype(jnp.int32) + 1

    def which(n):
        w = jnp.where(n >= HALO, 1, 0)
        return w, n - HALO * w

    def place(w, t):
        first = (corners_ref[w, 1] + t * CT) & (NG - 1)
        return first, first + CT > NG

    def chunk_range(w, j, t):
        first, wraps = place(w, t)
        last = first + CT - 1 + reach
        end_bucket = jnp.where(wraps, last - NG, jnp.minimum(last, NG - 1)) // BUCKET + 1
        start_bucket = jnp.maximum(first - reach, 0) // BUCKET
        starts = []
        passes = jnp.int32(1)
        for l in range(CUTS):
            i = CUTS * j + l
            start = off_ref[i, start_bucket] // CH
            end = jnp.where(end_bucket >= NG // BUCKET, NA, off_ref[i, jnp.minimum(end_bucket, NG // BUCKET - 1)])
            end = jnp.where(wraps, end + NA, end)
            chunks = jnp.minimum((end + CH - 1) // CH - start, NCH)
            passes = jnp.maximum(passes, (chunks + PASS - 1) // PASS)
            starts.append(start)
        return starts, passes

    def fill(w, j, t, starts, p, left, right):
        first, wraps = place(w, t)
        shift = corners_ref[w, 0] & (TR - 1)
        rows = ((iota((TR, 1), 0) + shift) & (TR - 1)).astype(F32)
        step = iota((CT, 1), 0)
        gap = jnp.where(step >= NG - first, GAP, 0)
        columns = jnp.broadcast_to((step - CT // 2 + gap).astype(F32), (CT, CH)).astype(BF16)
        origin = (first + CT // 2).astype(F32)
        beyond = jnp.where(wraps, NG // 2, -1).astype(F32)
        for l in range(CUTS):
            for m in range(PASS):
                chunk = (starts[l] + p * PASS + m) & (NCH - 1)
                at = pl.ds((CUTS * j + l) * NCH + chunk, 1)
                c = l * PASS + m
                fall = fall_ref[at, :]
                column = col_ref[at, :]
                column = column - origin + jnp.where(column < beyond, float(NG + GAP), 0.0)
                column = jnp.clip(column, -CLIP, CLIP)
                column16 = jnp.broadcast_to(column, (16, CH)).astype(BF16)
                fall16 = jnp.broadcast_to(fall, (16, CH)).astype(BF16)
                for s in range(CT // 16):
                    far = columns[16 * s : 16 * s + 16] - column16
                    right[c, 16 * s : 16 * s + 16, :] = jnp.exp2(far * far * fall16)
                far = rows - row_ref[at, :]
                profile = (str_ref[at, :] * jnp.exp2(far * far * fall)).astype(BF16)
                bins = jnp.broadcast_to(bin_ref[at, :], (16, CH))
                for k in range(SLICES):
                    mask = (bins == k).astype(F32).astype(BF16)
                    for s in range(TR // 16):
                        left[c, k * TR + 16 * s : k * TR + 16 * s + 16, :] = profile[16 * s : 16 * s + 16] * mask

    def product(left, right):
        wide = [jnp.concatenate([ref[c] for c in range(CUTS * PASS)], axis=1) for ref in (left, right)]
        return nt(*wide)

    def own_rows(w):
        return jnp.broadcast_to(iota((TR, 1), 0) + (corners_ref[w, 0] & (TR - 1)) < TR, (TR, CT))

    def store(w, j, t, value, keep=False):
        own = own_rows(w)
        lanes = pl.ds(t * CT, CT) if isinstance(t, int) else pl.ds(pl.multiple_of(t * CT, CT), CT)
        for k in range(SLICES):
            new = value[k * TR : (k + 1) * TR].astype(BF16)
            pot_ref[w, j, k, :, lanes] = jnp.where(own, pot_ref[w, j, k, :, lanes], new)
            if keep:
                new = jnp.where(own, new, pot_ref[w, j + 1, k, :, lanes])
            pot_ref[w, j + 1, k, :, lanes] = new

    def window_blocks(n, count):
        w, j = which(n)
        values = [product(left, right) for left, right in buffers]
        for t, (left, right) in enumerate(buffers):
            starts, passes = chunk_range(w, j, t)
            busy_ref[count] = tiles * n + t
            count = count + jnp.where(passes > 1, 1, 0)
            fill(w, j, t, starts, 0, left, right)
        before = which(jnp.maximum(n - 1, 0))
        for t, value in enumerate(values):
            store(*before, t, value)
        return count

    buffers = ((left0, right0), (left1, right1))
    count = lax.fori_loop(0, PB * HALO, window_blocks, jnp.int32(0))
    for t, (left, right) in enumerate(buffers):
        store(PB - 1, HALO - 1, t, product(left, right))

    def crowded(i, carry):
        entry = busy_ref[i]
        w, j = which(entry // tiles)
        t = entry & (tiles - 1)
        starts, passes = chunk_range(w, j, t)
        acc_ref[...] = jnp.zeros_like(acc_ref)

        def one_pass(p, carry):
            fill(w, j, t, starts, p, left0, right0)
            acc_ref[...] += product(left0, right0)
            return carry

        lax.fori_loop(0, passes, one_pass, 0)
        store(w, j, t, acc_ref[...], keep=True)
        return carry

    lax.fori_loop(0, count, crowded, 0)

    for fetch in fetches[4:]:
        fetch.wait()
    for b in range(NLB):
        n = min(LB, W - b * LB)
        turn = (TPAD - b * LB) % W
        for plane in range(2):
            rows = fresnel_ref[plane, b * LB : b * LB + n, :].astype(F32)
            block = pltpu.roll(rows, turn, 1)[:, :LK]
            if plane == 0:
                lw_ref[b, 0:n, 0:LK] = block.astype(BF16)
                lw_ref[b, LB : LB + n, LK : 2 * LK] = block.astype(BF16)
            else:
                lw_ref[b, 0:n, LK : 2 * LK] = (-block).astype(BF16)
                lw_ref[b, LB : LB + n, 0:LK] = block.astype(BF16)
    for b, (lo, hi) in enumerate(RIGHT_SPANS):
        k = hi - lo
        real = fresnel_ref[0, b * 128 : (b + 1) * 128, lo:hi]
        imag = fresnel_ref[1, b * 128 : (b + 1) * 128, lo:hi]
        rws[b][0:128, 0:k] = real
        rws[b][0:128, k : 2 * k] = -imag
        rws[b][128:256, 0:k] = imag
        rws[b][128:256, k : 2 * k] = real
    trans0[...] = jnp.zeros_like(trans0)
    trans1[...] = jnp.zeros_like(trans1)

    for w in range(PB):
        out_ref[w] = modes_ref[w].astype(F32)

    def transmit(w, k, trans, i):
        rows = slice(i * GR, (i + 1) * GR)
        block, part = i * GR // TR, i * GR % TR
        turns = pot_ref[w, block + 1, k, part : part + GR, :].astype(F32) * PHASE
        turns = turns - jnp.round(turns)
        square = turns * turns
        cosine = jnp.full_like(square, COS[-1])
        sine = jnp.full_like(square, SIN[-1])
        for a, b in zip(COS[-2::-1], SIN[-2::-1]):
            cosine = cosine * square + a
            sine = sine * square + b
        sine = sine * turns
        real = out_ref[w, 0, rows, :]
        imag = out_ref[w, 1, rows, :]
        into = slice(i * GR + TPAD, (i + 1) * GR + TPAD)
        trans[0, into, :] = (real * cosine - imag * sine).astype(BF16)
        trans[1, into, :] = (real * sine + imag * cosine).astype(BF16)

    def left_product(trans, half, b):
        n = min(LB, W - b * LB)
        rows = slice(b * LB, b * LB + LK)
        both = jnp.concatenate([trans[0, rows, :], trans[1, rows, :]], axis=0)
        product = nn(lw_ref[b], both).astype(BF16)
        half[0, b * LB : b * LB + n, :] = product[0:n]
        half[1, b * LB : b * LB + n, :] = product[LB : LB + n]

    def right_product(w, half, b):
        lo, hi = RIGHT_SPANS[b]
        both = jnp.concatenate([half[0, :, lo:hi], half[1, :, lo:hi]], axis=1)
        product = nt(both, rws[b][...])
        out_ref[w, 0, :, b * 128 : (b + 1) * 128] = product[:, :128]
        out_ref[w, 1, :, b * 128 : (b + 1) * 128] = product[:, 128:]

    def stage(right, left):
        spans = [functools.partial(right_product, *right, b) for b in range(4)] if right else []
        done = 0
        for b in range(NLB):
            if b < len(spans):
                spans[b]()
            if left:
                w, k, trans, half = left
                until = min(W // GR, -(-(b * LB + LK - TPAD) // GR))
                for i in range(done, until):
                    transmit(w, k, trans, i)
                done = until
                left_product(trans, half, b)

    def send(w):
        return pltpu.make_async_copy(out_ref.at[w], out_hbm.at[w], out_sems.at[w])

    stage(None, (0, 0, trans0, half0))

    def one_slice(k, carry):
        @pl.when(k < SLICES)
        def _():
            stage((0, half0), (1, k, trans1, half1))

        @pl.when(k < SLICES - 1)
        def _():
            stage((1, half1), (0, k + 1, trans0, half0))

        return carry

    lax.fori_loop(0, SLICES, one_slice, 0)
    send(0).start()
    stage((1, half1), None)
    send(1).start()
    for w in range(PB):
        send(w).wait()


def compute(corners, amp, width, lists, modes, fresnel):
    hbm = pl.BlockSpec(memory_space=pltpu.HBM)
    field = pltpu.VMEM((LISTS * NCH, CH), F32)
    return pl.pallas_call(
        compute_kernel,
        out_shape=jax.ShapeDtypeStruct((PB, 2, W, W), F32),
        in_specs=[hbm] * 6,
        out_specs=hbm,
        scratch_shapes=[
            pltpu.SMEM((PB, 2), jnp.int32),
            pltpu.SMEM((NSPEC,), F32),
            pltpu.SMEM((NSPEC,), F32),
            pltpu.VMEM((LISTS, PACK, CH), BF16),
            pltpu.VMEM((PB, 2, W, W), BF16),
            pltpu.VMEM((2, W, W), BF16),
            pltpu.VMEM((PB, 2, W, W), F32),
            field,
            field,
            field,
            field,
            field,
            pltpu.VMEM((LISTS, CH), jnp.int32),
            pltpu.SMEM((LISTS, CH), jnp.int32),
            pltpu.VMEM((CUTS * PASS, SLICES * TR, CH), BF16),
            pltpu.VMEM((CUTS * PASS, CT, CH), BF16),
            pltpu.VMEM((CUTS * PASS, SLICES * TR, CH), BF16),
            pltpu.VMEM((CUTS * PASS, CT, CH), BF16),
            pltpu.VMEM((SLICES * TR, CT), F32),
            pltpu.VMEM((PB, HALO + 1, SLICES, TR, W), BF16),
            pltpu.VMEM((2, TPAD + W + 80, W), BF16),
            pltpu.VMEM((2, TPAD + W + 80, W), BF16),
            pltpu.VMEM((2, W, W), BF16),
            pltpu.VMEM((2, W, W), BF16),
            pltpu.VMEM((NLB, 2 * LB, 2 * LK), BF16),
        ]
        + [pltpu.VMEM((256, 2 * (hi - lo)), BF16) for lo, hi in RIGHT_SPANS]
        + [pltpu.SemaphoreType.DMA, pltpu.SMEM((PB * HALO * 2 + 1,), jnp.int32), pltpu.SemaphoreType.DMA((6,)), pltpu.SemaphoreType.DMA((PB,))],
        compiler_params=pltpu.CompilerParams(vmem_limit_bytes=60 * 1024 * 1024),
        name="windows_and_slices",
    )(corners, amp, width, lists, modes, fresnel)


def gather_lists(cells, bins, species):
    vmem = pl.BlockSpec(memory_space=pltpu.VMEM)
    passed = HALO * 2
    return pl.pallas_call(
        lists_kernel,
        out_shape=jax.ShapeDtypeStruct((LISTS, PACK, CH), BF16),
        in_specs=[vmem, vmem, vmem],
        out_specs=pl.BlockSpec(memory_space=pltpu.HBM),
        scratch_shapes=[
            pltpu.VMEM((PACK, CH), BF16),
            pltpu.SemaphoreType.DMA,
            pltpu.SemaphoreType.DMA((passed,)),
            pltpu.SemaphoreType.DMA((passed,)),
            pltpu.SemaphoreType.DMA((LISTS,)),
        ],
        compiler_params=pltpu.CompilerParams(collective_id=0, has_side_effects=True),
        name="sort_and_gather",
    )(cells, bins, species)


def body(
    probe_modes,
    probe_corners,
    atom_cells,
    atom_bins,
    atom_species,
    species_amp,
    species_width,
    fresnel,
):
    lists = gather_lists(atom_cells.T, atom_bins.T, atom_species.reshape(1, -1))
    return compute(probe_corners, species_amp, species_width, lists, probe_modes, fresnel)


def solution(mesh):
    return jax.shard_map(
        body,
        mesh=mesh,
        in_specs=(
            P(("cuts", "probe"), None, None, None),
            P(("cuts", "probe"), None),
            P(("cuts", "probe"), None),
            P(("cuts", "probe"), None),
            P(("cuts", "probe")),
            P(),
            P(),
            P(),
        ),
        out_specs=P(("cuts", "probe"), None, None, None),
        check_vma=False,
    )
```

```python
import functools

import jax
import jax.numpy as jnp
from jax import lax
from jax.experimental import pallas as pl
from jax.experimental.pallas import tpu as pltpu
from jax.sharding import PartitionSpec as P

NG = 2048
W = 512
TR = 64
NSPEC = 4
NA = 2048
SLICES = 4
CUTS = 4
PROBE = 32
PB = 2

HALO = 9
LISTS = HALO * CUTS
CH = 128
NCH = NA // CH
BUCKET = 16
FIELDS = 4
PACK = FIELDS * NCH
TILES = 2
UNPACK = 12
REACH = 13.7
CT = 256
GAP = 32
CLIP = 224.0
PASS = 4
HEAD = 176
TAIL = 128
SPANS = ((0, HEAD), (0, CT), (0, CT), (TAIL, CT))
MESH = pl.DeviceIdType.MESH
F32 = jnp.float32
BF16 = jnp.bfloat16

PHASE = 0.4 / 6.283185307179586
COS = (
    0.9999590208378119,
    -19.73094236686191,
    64.67144177616537,
    -82.390806311774,
    45.62105110286101,
)
SIN = (
    6.2831611294861265,
    -41.3368318308275,
    81.44770647022538,
    -74.90941970419655,
    33.548355145172366,
)


def nn(a, b):
    return lax.dot_general(a, b, (((1,), (0,)), ((), ())), preferred_element_type=F32)


def nt(a, b):
    return lax.dot_general(a, b, (((1,), (1,)), ((), ())), preferred_element_type=F32)


def iota(shape, dim):
    return lax.broadcasted_iota(jnp.int32, shape, dim)


def sort_into(cells_ref, bins_ref, species_ref, out_ref):
    before = (iota((CH, CH), 0) < iota((CH, CH), 1)).astype(F32).astype(BF16)
    below = (iota((CH, CH), 1) < iota((CH, CH), 0)).astype(F32).astype(BF16)
    ones = jnp.ones((CH, CH), BF16)
    buckets = iota((CH, CH), 0)
    hots = []
    prefixes = []
    running = jnp.zeros((CH, CH), F32)
    for c in range(NCH):
        lanes = slice(c * CH, (c + 1) * CH)
        column = cells_ref[1:2, lanes]
        hot = (buckets == column // BUCKET).astype(F32)
        hot16 = hot.astype(BF16)
        prefixes.append(nn(hot16, before) + running)
        running = running + nn(hot16, ones)
        hots.append(hot)
    high = jnp.floor(running * (1.0 / 64.0))
    low = running - 64.0 * high
    offset = 64.0 * nn(below, high.astype(BF16)) + nn(below, low.astype(BF16))
    sorted_fields = jnp.zeros((5 * NCH, CH), F32)
    for c in range(NCH):
        lanes = slice(c * CH, (c + 1) * CH)
        rank = jnp.sum(hots[c] * (prefixes[c] + offset), axis=0, keepdims=True).astype(jnp.int32)
        row = cells_ref[0:1, lanes] & (TR - 1)
        column = cells_ref[1:2, lanes]
        fields = (row, column // 64, column & 63, species_ref[0:1, lanes], bins_ref[0:1, lanes])
        chosen = (iota((NCH, CH), 0) == rank // CH).astype(F32)
        left = jnp.concatenate([chosen * f.astype(F32) for f in fields], axis=0).astype(BF16)
        right = (buckets == (rank & (CH - 1))).astype(F32).astype(BF16)
        sorted_fields = sorted_fields + nt(left, right)
    row, high, low, kind, bins = [sorted_fields[f * NCH : (f + 1) * NCH] for f in range(5)]
    for f, field in enumerate((row, 64.0 * high + low, kind, bins)):
        out_ref[f * NCH : (f + 1) * NCH, :] = field.astype(jnp.int32).astype(jnp.int16)


def lists_kernel(cells_ref, bins_ref, species_ref, out_ref, own_ref, local_sem, send_sems, pass_sems, recv_sems):
    g = lax.axis_index("cuts")
    q = lax.axis_index("probe")
    core = lax.rem(g, 2)
    sibling = (g + 1 - 2 * core, q)
    barrier = pltpu.get_barrier_semaphore()
    pairs = [(j, r) for j in (1, 2, 0, 3, 4, 5, 6, 7, 8) for r in (0, 2) if (j, r) != (1, 0)]

    def holder(j, r):
        return lax.rem(g + r, CUTS), lax.rem(q + j - 1 + PROBE, PROBE)

    def reader(j, r):
        return lax.rem(g + r, CUTS), lax.rem(q + 1 - j + PROBE, PROBE)

    def remote(src, slot, send_sem, device):
        return pltpu.make_async_remote_copy(
            src_ref=src,
            dst_ref=out_ref.at[slot],
            send_sem=send_sem,
            recv_sem=recv_sems.at[slot],
            device_id=device,
            device_id_type=MESH,
        )

    pl.semaphore_signal(barrier, inc=1, device_id=sibling, device_id_type=MESH)
    for j, r in pairs:
        pl.semaphore_signal(barrier, inc=1, device_id=holder(j, r), device_id_type=MESH)
    sort_into(cells_ref, bins_ref, species_ref, own_ref)
    local = pltpu.make_async_copy(own_ref, out_ref.at[CUTS + g], local_sem)
    local.start()
    pl.semaphore_wait(barrier, len(pairs) + 1)
    sends = []
    for n, (j, r) in enumerate(pairs):
        sends.append(remote(own_ref, CUTS * j + g, send_sems.at[n], reader(j, r)))
    sends.append(remote(own_ref, CUTS + g, pass_sems.at[len(pairs)], sibling))
    for copy in sends:
        copy.start()
    for n, (j, r) in enumerate(pairs):
        slot = CUTS * j + lax.rem(g + r, CUTS)
        remote(own_ref, slot, send_sems.at[n], sibling).wait_recv()
        onward = remote(out_ref.at[slot], slot, pass_sems.at[n], sibling)
        onward.start()
        sends.append(onward)
    for j in range(HALO):
        for r in (1, 3):
            slot = CUTS * j + lax.rem(g + r, CUTS)
            remote(own_ref, slot, send_sems.at[0], sibling).wait_recv()
    for copy in sends:
        copy.wait_send()
    local.wait()


GR = 32
LB = 96
LK = 128
NLB = -(-W // LB)
TPAD = 16
RIGHT_SPANS = ((0, 256), (0, 384), (128, 512), (256, 512))


def compute_kernel(
    corners_hbm,
    amp_hbm,
    width_hbm,
    lists_hbm,
    modes_hbm,
    fresnel_hbm,
    out_hbm,
    corners_ref,
    amp_ref,
    width_ref,
    lists_ref,
    modes_ref,
    fresnel_ref,
    out_ref,
    col_ref,
    fall_ref,
    row_ref,
    str_ref,
    bin_ref,
    count_vec,
    count_ref,
    left0,
    right0,
    left1,
    right1,
    acc_ref,
    pot_ref,
    trans0,
    trans1,
    half0,
    half1,
    lw_ref,
    rw0,
    rw1,
    rw2,
    rw3,
    sem,
    busy_ref,
    in_sems,
    out_sems,
):
    rws = (rw0, rw1, rw2, rw3)
    sources = (lists_hbm, corners_hbm, amp_hbm, width_hbm, fresnel_hbm, modes_hbm)
    targets = (lists_ref, corners_ref, amp_ref, width_ref, fresnel_ref, modes_ref)
    fetches = [pltpu.make_async_copy(a, b, in_sems.at[n]) for n, (a, b) in enumerate(zip(sources, targets))]
    for fetch in fetches:
        fetch.start()
    for fetch in fetches[:4]:
        fetch.wait()

    widest = width_ref[0]
    for species in range(1, NSPEC):
        widest = jnp.maximum(widest, width_ref[species])
    reach = (widest * REACH).astype(jnp.int32) + 1

    def which(n):
        w = jnp.where(n >= HALO, 1, 0)
        return w, n - HALO * w

    def place(w, t):
        first = (corners_ref[w, 1] + t * CT) & (NG - 1)
        return first, first + CT > NG

    def buckets_of(w, t):
        first, wraps = place(w, t)
        most = jnp.where(wraps, 2 * NG, NG) // BUCKET
        last = first + CT - 1 + reach
        return (
            jnp.maximum(first - reach, 0) // BUCKET,
            (first + HEAD - reach) // BUCKET,
            jnp.minimum(last // BUCKET + 1, most),
            jnp.minimum((first + TAIL + reach + BUCKET - 1) // BUCKET, most),
        )

    lane = iota((1, CH), 1)
    edge = jnp.zeros((1, CH), jnp.int32)
    for n in range(PB * TILES):
        for kind, bucket in enumerate(buckets_of(n // TILES, n % TILES)):
            bucket = jnp.where(bucket > NG // BUCKET, bucket - NG // BUCKET, bucket)
            edge = jnp.where(lane == 4 * kind + n, bucket * BUCKET, edge)
    edge = jnp.broadcast_to(edge.astype(F32), (NCH, CH))
    by_tail = iota((NCH, CH), 1) < 8

    def unpack_list(i):
        def part(f):
            return lists_ref[i, f * NCH : (f + 1) * NCH, :].astype(jnp.int32)

        species = part(2)
        amp = jnp.zeros((NCH, CH), F32)
        width = jnp.zeros((NCH, CH), F32)
        for s in range(NSPEC):
            amp = jnp.where(species == s, amp_ref[s], amp)
            width = jnp.where(species == s, width_ref[s], width)
        column = part(1).astype(F32)
        rows = pl.ds(pl.multiple_of(i * NCH, NCH), NCH)
        row_ref[rows, :] = part(0).astype(F32)
        col_ref[rows, :] = column
        fall_ref[rows, :] = -0.7213475204444817 / (width * width)
        str_ref[rows, :] = amp
        bin_ref[rows, :] = part(3).astype(F32)
        tail = jnp.broadcast_to(column[:, CH - 1 : CH], (NCH, CH))
        head = jnp.broadcast_to(column[:, 0:1], (NCH, CH))
        below = (jnp.where(by_tail, tail, head) < edge).astype(F32)
        count_vec[pl.ds(i, 1), :] = jnp.sum(below, axis=0, keepdims=True).astype(jnp.int32)

    def unpack(n, carry):
        for l in range(UNPACK):
            unpack_list(UNPACK * n + l)
        return carry

    lax.fori_loop(0, LISTS // UNPACK, unpack, 0)
    copy = pltpu.make_async_copy(count_vec, count_ref, sem)
    copy.start()
    copy.wait()
    def chunk_range(w, j, t):
        around = [jnp.where(bucket > NG // BUCKET, NCH, 0) for bucket in buckets_of(w, t)]
        starts = []
        most = jnp.int32(0)
        long = jnp.int32(0)
        for l in range(CUTS):
            start, head, end, tail = [
                count_ref[CUTS * j + l, 4 * kind + TILES * w + t] + around[kind] for kind in range(4)
            ]
            most = jnp.maximum(most, jnp.minimum(end - start, NCH))
            short = (start + 1 <= head) & (start + PASS - 1 >= tail)
            long = jnp.maximum(long, jnp.where(short, 0, 1))
            starts.append(start)
        return starts, most, long

    def fill(w, j, t, starts, steps, left, right, spans=None):
        first, wraps = place(w, t)
        shift = corners_ref[w, 0] & (TR - 1)
        rows = jnp.broadcast_to(((iota((TR, 1), 0) + shift) & (TR - 1)).astype(F32), (TR, CH)).astype(BF16)
        step = iota((CT, 1), 0)
        gap = jnp.where(step >= NG - first, GAP, 0)
        columns = jnp.broadcast_to((step - CT // 2 + gap).astype(F32), (CT, CH)).astype(BF16)
        origin = (first + CT // 2).astype(F32)
        beyond = jnp.where(wraps, NG // 2, -1).astype(F32)
        for l in range(CUTS):
            for n, m in enumerate(steps):
                chunk = (starts[l] + m) & (NCH - 1)
                at = pl.ds((CUTS * j + l) * NCH + chunk, 1)
                c = l * len(steps) + n
                fall = fall_ref[at, :]
                column = col_ref[at, :]
                column = column - origin + jnp.where(column < beyond, float(NG + GAP), 0.0)
                column = jnp.clip(column, -CLIP, CLIP)
                column16 = jnp.broadcast_to(column, (16, CH)).astype(BF16)
                fall16 = jnp.broadcast_to(fall, (16, CH)).astype(BF16)
                low, high = spans[n] if spans else (0, CT)
                for s in range(low // 16, high // 16):
                    far = columns[16 * s : 16 * s + 16] - column16
                    right[c, 16 * s : 16 * s + 16, :] = jnp.exp2(far * far * fall16)
                row16 = jnp.broadcast_to(row_ref[at, :], (16, CH)).astype(BF16)
                profile = []
                for s in range(TR // 16):
                    far = rows[16 * s : 16 * s + 16] - row16
                    profile.append(jnp.exp2(far * far * fall16))
                bins = jnp.broadcast_to(bin_ref[at, :], (8, CH))
                strength = jnp.broadcast_to(str_ref[at, :], (8, CH))
                for k in range(SLICES):
                    scale = jnp.where(bins == k, strength, 0.0)
                    scale = jnp.concatenate([scale, scale], axis=0).astype(BF16)
                    for s in range(TR // 16):
                        left[c, k * TR + 16 * s : k * TR + 16 * s + 16, :] = profile[s] * scale

    def product(left, right, chunks=CUTS * PASS):
        wide = [jnp.concatenate([ref[c] for c in range(chunks)], axis=1) for ref in (left, right)]
        return nt(*wide)

    def own_rows(w):
        return jnp.broadcast_to(iota((TR, 1), 0) + (corners_ref[w, 0] & (TR - 1)) < TR, (TR, CT))

    def store(w, j, t, value, keep=False):
        own = own_rows(w)
        lanes = pl.ds(t * CT, CT) if isinstance(t, int) else pl.ds(pl.multiple_of(t * CT, CT), CT)
        for k in range(SLICES):
            new = value[k * TR : (k + 1) * TR].astype(BF16)
            pot_ref[w, j, k, :, lanes] = jnp.where(own, pot_ref[w, j, k, :, lanes], new)
            if keep:
                new = jnp.where(own, new, pot_ref[w, j + 1, k, :, lanes])
            pot_ref[w, j + 1, k, :, lanes] = new

    def window_blocks(n, count):
        w, j = which(n)
        values = [product(left, right) for left, right in buffers]
        for t, (left, right) in enumerate(buffers):
            starts, most, long = chunk_range(w, j, t)
            busy_ref[count] = TILES * n + t
            count = count + jnp.where(most > PASS, 1, long)
            fill(w, j, t, starts, range(PASS), left, right, SPANS)
        before = which(jnp.maximum(n - 1, 0))
        for t, value in enumerate(values):
            store(*before, t, value)
        return count

    buffers = ((left0, right0), (left1, right1))
    for _, right in buffers:
        for c in range(CUTS * PASS):
            low, high = SPANS[c % PASS]
            if low > 0:
                right[c, 0:low, :] = jnp.zeros((low, CH), BF16)
            if high < CT:
                right[c, high:CT, :] = jnp.zeros((CT - high, CH), BF16)
    count = lax.fori_loop(0, PB * HALO, window_blocks, jnp.int32(0))
    for t, (left, right) in enumerate(buffers):
        store(PB - 1, HALO - 1, t, product(left, right))

    def crowded(i, carry):
        entry = busy_ref[i]
        w, j = which(entry // TILES)
        t = entry & (TILES - 1)
        starts, most, _ = chunk_range(w, j, t)
        fill(w, j, t, starts, range(PASS), left0, right0)
        acc_ref[...] = product(left0, right0)

        def one_more(m, carry):
            fill(w, j, t, starts, [m], left0, right0)
            acc_ref[...] += product(left0, right0, CUTS)
            return carry

        lax.fori_loop(PASS, jnp.maximum(most, PASS), one_more, 0)
        store(w, j, t, acc_ref[...], keep=True)
        return carry

    lax.fori_loop(0, count, crowded, 0)

    for fetch in fetches[4:]:
        fetch.wait()
    for b in range(NLB):
        n = min(LB, W - b * LB)
        turn = (TPAD - b * LB) % W
        for plane in range(2):
            rows = fresnel_ref[plane, b * LB : b * LB + n, :].astype(F32)
            block = pltpu.roll(rows, turn, 1)[:, :LK]
            if plane == 0:
                lw_ref[b, 0:n, 0:LK] = block.astype(BF16)
                lw_ref[b, LB : LB + n, LK : 2 * LK] = block.astype(BF16)
            else:
                lw_ref[b, 0:n, LK : 2 * LK] = (-block).astype(BF16)
                lw_ref[b, LB : LB + n, 0:LK] = block.astype(BF16)
    for b, (lo, hi) in enumerate(RIGHT_SPANS):
        k = hi - lo
        real = fresnel_ref[0, b * 128 : (b + 1) * 128, lo:hi]
        imag = fresnel_ref[1, b * 128 : (b + 1) * 128, lo:hi]
        rws[b][0:128, 0:k] = real
        rws[b][0:128, k : 2 * k] = -imag
        rws[b][128:256, 0:k] = imag
        rws[b][128:256, k : 2 * k] = real
    trans0[...] = jnp.zeros_like(trans0)
    trans1[...] = jnp.zeros_like(trans1)

    for w in range(PB):
        out_ref[w] = modes_ref[w].astype(F32)

    def transmit(w, k, trans, i):
        rows = slice(i * GR, (i + 1) * GR)
        block, part = i * GR // TR, i * GR % TR
        turns = pot_ref[w, block + 1, k, part : part + GR, :].astype(F32) * PHASE
        turns = turns - jnp.round(turns)
        square = turns * turns
        cosine = jnp.full_like(square, COS[-1])
        sine = jnp.full_like(square, SIN[-1])
        for a, b in zip(COS[-2::-1], SIN[-2::-1]):
            cosine = cosine * square + a
            sine = sine * square + b
        sine = sine * turns
        real = out_ref[w, 0, rows, :]
        imag = out_ref[w, 1, rows, :]
        into = slice(i * GR + TPAD, (i + 1) * GR + TPAD)
        trans[0, into, :] = (real * cosine - imag * sine).astype(BF16)
        trans[1, into, :] = (real * sine + imag * cosine).astype(BF16)

    def left_product(trans, half, b):
        n = min(LB, W - b * LB)
        rows = slice(b * LB, b * LB + LK)
        both = jnp.concatenate([trans[0, rows, :], trans[1, rows, :]], axis=0)
        product = nn(lw_ref[b], both).astype(BF16)
        half[0, b * LB : b * LB + n, :] = product[0:n]
        half[1, b * LB : b * LB + n, :] = product[LB : LB + n]

    def right_product(w, half, b):
        lo, hi = RIGHT_SPANS[b]
        both = jnp.concatenate([half[0, :, lo:hi], half[1, :, lo:hi]], axis=1)
        product = nt(both, rws[b][...])
        out_ref[w, 0, :, b * 128 : (b + 1) * 128] = product[:, :128]
        out_ref[w, 1, :, b * 128 : (b + 1) * 128] = product[:, 128:]

    def stage(right, left):
        spans = [functools.partial(right_product, *right, b) for b in range(4)] if right else []
        done = 0
        for b in range(NLB):
            if b < len(spans):
                spans[b]()
            if left:
                w, k, trans, half = left
                until = min(W // GR, -(-(b * LB + LK - TPAD) // GR))
                for i in range(done, until):
                    transmit(w, k, trans, i)
                done = until
                left_product(trans, half, b)

    def send(w):
        return pltpu.make_async_copy(out_ref.at[w], out_hbm.at[w], out_sems.at[w])

    stage(None, (0, 0, trans0, half0))

    def one_slice(k, carry):
        @pl.when(k < SLICES)
        def _():
            stage((0, half0), (1, k, trans1, half1))

        @pl.when(k < SLICES - 1)
        def _():
            stage((1, half1), (0, k + 1, trans0, half0))

        return carry

    lax.fori_loop(0, SLICES, one_slice, 0)
    send(0).start()
    stage((1, half1), None)
    send(1).start()
    for w in range(PB):
        send(w).wait()


def compute(corners, amp, width, lists, modes, fresnel):
    hbm = pl.BlockSpec(memory_space=pltpu.HBM)
    field = pltpu.VMEM((LISTS * NCH, CH), F32)
    return pl.pallas_call(
        compute_kernel,
        out_shape=jax.ShapeDtypeStruct((PB, 2, W, W), F32),
        in_specs=[hbm] * 6,
        out_specs=hbm,
        scratch_shapes=[
            pltpu.SMEM((PB, 2), jnp.int32),
            pltpu.SMEM((NSPEC,), F32),
            pltpu.SMEM((NSPEC,), F32),
            pltpu.VMEM((LISTS, PACK, CH), jnp.int16),
            pltpu.VMEM((PB, 2, W, W), BF16),
            pltpu.VMEM((2, W, W), BF16),
            pltpu.VMEM((PB, 2, W, W), F32),
            field,
            field,
            field,
            field,
            field,
            pltpu.VMEM((LISTS, CH), jnp.int32),
            pltpu.SMEM((LISTS, CH), jnp.int32),
            pltpu.VMEM((CUTS * PASS, SLICES * TR, CH), BF16),
            pltpu.VMEM((CUTS * PASS, CT, CH), BF16),
            pltpu.VMEM((CUTS * PASS, SLICES * TR, CH), BF16),
            pltpu.VMEM((CUTS * PASS, CT, CH), BF16),
            pltpu.VMEM((SLICES * TR, CT), F32),
            pltpu.VMEM((PB, HALO + 1, SLICES, TR, W), BF16),
            pltpu.VMEM((2, TPAD + W + 80, W), BF16),
            pltpu.VMEM((2, TPAD + W + 80, W), BF16),
            pltpu.VMEM((2, W, W), BF16),
            pltpu.VMEM((2, W, W), BF16),
            pltpu.VMEM((NLB, 2 * LB, 2 * LK), BF16),
        ]
        + [pltpu.VMEM((256, 2 * (hi - lo)), BF16) for lo, hi in RIGHT_SPANS]
        + [pltpu.SemaphoreType.DMA, pltpu.SMEM((PB * HALO * 2 + 1,), jnp.int32), pltpu.SemaphoreType.DMA((6,)), pltpu.SemaphoreType.DMA((PB,))],
        compiler_params=pltpu.CompilerParams(vmem_limit_bytes=60 * 1024 * 1024),
        name="windows_and_slices",
    )(corners, amp, width, lists, modes, fresnel)


def gather_lists(cells, bins, species):
    vmem = pl.BlockSpec(memory_space=pltpu.VMEM)
    passed = HALO * 2
    return pl.pallas_call(
        lists_kernel,
        out_shape=jax.ShapeDtypeStruct((LISTS, PACK, CH), jnp.int16),
        in_specs=[vmem, vmem, vmem],
        out_specs=pl.BlockSpec(memory_space=pltpu.HBM),
        scratch_shapes=[
            pltpu.VMEM((PACK, CH), jnp.int16),
            pltpu.SemaphoreType.DMA,
            pltpu.SemaphoreType.DMA((passed,)),
            pltpu.SemaphoreType.DMA((passed,)),
            pltpu.SemaphoreType.DMA((LISTS,)),
        ],
        compiler_params=pltpu.CompilerParams(collective_id=0, has_side_effects=True),
        name="sort_and_gather",
    )(cells, bins, species)


def body(
    probe_modes,
    probe_corners,
    atom_cells,
    atom_bins,
    atom_species,
    species_amp,
    species_width,
    fresnel,
):
    lists = gather_lists(atom_cells.T, atom_bins.T, atom_species.reshape(1, -1))
    return compute(probe_corners, species_amp, species_width, lists, probe_modes, fresnel)


def solution(mesh):
    return jax.shard_map(
        body,
        mesh=mesh,
        in_specs=(
            P(("cuts", "probe"), None, None, None),
            P(("cuts", "probe"), None),
            P(("cuts", "probe"), None),
            P(("cuts", "probe"), None),
            P(("cuts", "probe")),
            P(),
            P(),
            P(),
        ),
        out_specs=P(("cuts", "probe"), None, None, None),
        check_vma=False,
    )
```

```python
import functools

import jax
import jax.numpy as jnp
from jax import lax
from jax.experimental import pallas as pl
from jax.experimental.pallas import tpu as pltpu
from jax.sharding import PartitionSpec as P

NG = 2048
W = 512
TR = 64
NSPEC = 4
NA = 2048
SLICES = 4
CUTS = 4
PROBE = 32
PB = 2

HALO = 9
LISTS = HALO * CUTS
CH = 128
NCH = NA // CH
BUCKET = 16
FIELDS = 4
PACK = FIELDS * NCH
TILES = 2
UNPACK = 12
REACH = 13.7
CT = 256
GAP = 32
CLIP = 224.0
PASS = 4
HEAD = 176
TAIL = 128
SPANS = ((0, HEAD), (0, CT), (0, CT), (TAIL, CT))
MESH = pl.DeviceIdType.MESH
F32 = jnp.float32
BF16 = jnp.bfloat16

PHASE = 0.4 / 6.283185307179586
COS = (
    0.9999590208378119,
    -19.73094236686191,
    64.67144177616537,
    -82.390806311774,
    45.62105110286101,
)
SIN = (
    6.2831611294861265,
    -41.3368318308275,
    81.44770647022538,
    -74.90941970419655,
    33.548355145172366,
)


def nn(a, b):
    return lax.dot_general(a, b, (((1,), (0,)), ((), ())), preferred_element_type=F32)


def nt(a, b):
    return lax.dot_general(a, b, (((1,), (1,)), ((), ())), preferred_element_type=F32)


def iota(shape, dim):
    return lax.broadcasted_iota(jnp.int32, shape, dim)


def sort_into(cells_ref, bins_ref, species_ref, out_ref):
    before = (iota((CH, CH), 0) < iota((CH, CH), 1)).astype(F32).astype(BF16)
    below = (iota((CH, CH), 1) < iota((CH, CH), 0)).astype(F32).astype(BF16)
    ones = jnp.ones((CH, CH), BF16)
    buckets = iota((CH, CH), 0)
    chunks = [slice(c * CH, (c + 1) * CH) for c in range(NCH)]
    hots = [(buckets == cells_ref[1:2, lanes] // BUCKET).astype(F32) for lanes in chunks]
    tall = jnp.concatenate([hot.astype(BF16) for hot in hots], axis=0)
    sums = nn(tall, jnp.concatenate([before, ones], axis=1))
    running = jnp.zeros((CH, CH), F32)
    prefixes = []
    for lanes in chunks:
        prefixes.append(sums[lanes, :CH] + running)
        running = running + sums[lanes, CH:]
    high = jnp.floor(running * (1.0 / 64.0))
    low = running - 64.0 * high
    offset = 64.0 * nn(below, high.astype(BF16)) + nn(below, low.astype(BF16))
    lefts = []
    rights = []
    for lanes, hot, prefix in zip(chunks, hots, prefixes):
        rank = jnp.sum(hot * (prefix + offset), axis=0, keepdims=True).astype(jnp.int32)
        row = cells_ref[0:1, lanes] & (TR - 1)
        column = cells_ref[1:2, lanes]
        fields = (row, column // 64, column & 63, species_ref[0:1, lanes], bins_ref[0:1, lanes])
        chosen = (iota((NCH, CH), 0) == rank // CH).astype(F32)
        lefts.append(jnp.concatenate([chosen * f.astype(F32) for f in fields], axis=0).astype(BF16))
        rights.append((buckets == (rank & (CH - 1))).astype(F32).astype(BF16))
    sorted_fields = nt(jnp.concatenate(lefts, axis=1), jnp.concatenate(rights, axis=1))
    row, high, low, kind, bins = [sorted_fields[f * NCH : (f + 1) * NCH] for f in range(5)]
    for f, field in enumerate((row, 64.0 * high + low, kind, bins)):
        out_ref[f * NCH : (f + 1) * NCH, :] = field.astype(jnp.int32).astype(jnp.int16)


def lists_kernel(cells_ref, bins_ref, species_ref, out_ref, own_ref, local_sem, send_sems, pass_sems, recv_sems):
    g = lax.axis_index("cuts")
    q = lax.axis_index("probe")
    core = lax.rem(g, 2)
    sibling = (g + 1 - 2 * core, q)
    barrier = pltpu.get_barrier_semaphore()
    pairs = [(j, r) for j in (1, 2, 0, 3, 4, 5, 6, 7, 8) for r in (0, 2) if (j, r) != (1, 0)]

    def holder(j, r):
        return lax.rem(g + r, CUTS), lax.rem(q + j - 1 + PROBE, PROBE)

    def reader(j, r):
        return lax.rem(g + r, CUTS), lax.rem(q + 1 - j + PROBE, PROBE)

    def remote(src, slot, send_sem, device):
        return pltpu.make_async_remote_copy(
            src_ref=src,
            dst_ref=out_ref.at[slot],
            send_sem=send_sem,
            recv_sem=recv_sems.at[slot],
            device_id=device,
            device_id_type=MESH,
        )

    pl.semaphore_signal(barrier, inc=1, device_id=sibling, device_id_type=MESH)
    for j, r in pairs:
        pl.semaphore_signal(barrier, inc=1, device_id=holder(j, r), device_id_type=MESH)
    sort_into(cells_ref, bins_ref, species_ref, own_ref)
    local = pltpu.make_async_copy(own_ref, out_ref.at[CUTS + g], local_sem)
    local.start()
    pl.semaphore_wait(barrier, len(pairs) + 1)
    sends = []
    for n, (j, r) in enumerate(pairs):
        sends.append(remote(own_ref, CUTS * j + g, send_sems.at[n], reader(j, r)))
    sends.append(remote(own_ref, CUTS + g, pass_sems.at[len(pairs)], sibling))
    for copy in sends:
        copy.start()
    for n, (j, r) in enumerate(pairs):
        slot = CUTS * j + lax.rem(g + r, CUTS)
        remote(own_ref, slot, send_sems.at[n], sibling).wait_recv()
        onward = remote(out_ref.at[slot], slot, pass_sems.at[n], sibling)
        onward.start()
        sends.append(onward)
    for j in range(HALO):
        for r in (1, 3):
            slot = CUTS * j + lax.rem(g + r, CUTS)
            remote(own_ref, slot, send_sems.at[0], sibling).wait_recv()
    for copy in sends:
        copy.wait_send()
    local.wait()


GR = 32
LB = 96
LK = 128
NLB = -(-W // LB)
TPAD = 16
RIGHT_SPANS = ((0, 256), (0, 384), (128, 512), (256, 512))


def compute_kernel(
    corners_hbm,
    amp_hbm,
    width_hbm,
    lists_hbm,
    modes_hbm,
    fresnel_hbm,
    out_hbm,
    corners_ref,
    amp_ref,
    width_ref,
    lists_ref,
    modes_ref,
    fresnel_ref,
    out_ref,
    col_ref,
    fall_ref,
    row_ref,
    str_ref,
    bin_ref,
    count_vec,
    count_ref,
    left0,
    right0,
    left1,
    right1,
    acc_ref,
    pot_ref,
    trans0,
    trans1,
    half0,
    half1,
    lw_ref,
    rw0,
    rw1,
    rw2,
    rw3,
    sem,
    busy_ref,
    in_sems,
    out_sems,
):
    rws = (rw0, rw1, rw2, rw3)
    sources = (lists_hbm, corners_hbm, amp_hbm, width_hbm, fresnel_hbm, modes_hbm)
    targets = (lists_ref, corners_ref, amp_ref, width_ref, fresnel_ref, modes_ref)
    fetches = [pltpu.make_async_copy(a, b, in_sems.at[n]) for n, (a, b) in enumerate(zip(sources, targets))]
    for fetch in fetches:
        fetch.start()
    for fetch in fetches[:4]:
        fetch.wait()

    widest = width_ref[0]
    for species in range(1, NSPEC):
        widest = jnp.maximum(widest, width_ref[species])
    reach = (widest * REACH).astype(jnp.int32) + 1

    def which(n):
        w = jnp.where(n >= HALO, 1, 0)
        return w, n - HALO * w

    def place(w, t):
        first = (corners_ref[w, 1] + t * CT) & (NG - 1)
        return first, first + CT > NG

    def buckets_of(w, t):
        first, wraps = place(w, t)
        most = jnp.where(wraps, 2 * NG, NG) // BUCKET
        last = first + CT - 1 + reach
        return (
            jnp.maximum(first - reach, 0) // BUCKET,
            (first + HEAD - reach) // BUCKET,
            jnp.minimum(last // BUCKET + 1, most),
            jnp.minimum((first + TAIL + reach + BUCKET - 1) // BUCKET, most),
        )

    lane = iota((1, CH), 1)
    edge = jnp.zeros((1, CH), jnp.int32)
    for n in range(PB * TILES):
        for kind, bucket in enumerate(buckets_of(n // TILES, n % TILES)):
            bucket = jnp.where(bucket > NG // BUCKET, bucket - NG // BUCKET, bucket)
            edge = jnp.where(lane == 4 * kind + n, bucket * BUCKET, edge)
    edge = jnp.broadcast_to(edge.astype(F32), (NCH, CH))
    by_tail = iota((NCH, CH), 1) < 8

    def unpack_list(i):
        def part(f):
            return lists_ref[i, f * NCH : (f + 1) * NCH, :].astype(jnp.int32)

        species = part(2)
        amp = jnp.zeros((NCH, CH), F32)
        width = jnp.zeros((NCH, CH), F32)
        for s in range(NSPEC):
            amp = jnp.where(species == s, amp_ref[s], amp)
            width = jnp.where(species == s, width_ref[s], width)
        column = part(1).astype(F32)
        rows = pl.ds(pl.multiple_of(i * NCH, NCH), NCH)
        row_ref[rows, :] = part(0).astype(F32)
        col_ref[rows, :] = column
        fall_ref[rows, :] = -0.7213475204444817 / (width * width)
        str_ref[rows, :] = amp
        bin_ref[rows, :] = part(3).astype(F32)
        tail = jnp.broadcast_to(column[:, CH - 1 : CH], (NCH, CH))
        head = jnp.broadcast_to(column[:, 0:1], (NCH, CH))
        below = (jnp.where(by_tail, tail, head) < edge).astype(F32)
        count_vec[pl.ds(i, 1), :] = jnp.sum(below, axis=0, keepdims=True).astype(jnp.int32)

    def unpack(n, carry):
        for l in range(UNPACK):
            unpack_list(UNPACK * n + l)
        return carry

    lax.fori_loop(0, LISTS // UNPACK, unpack, 0)
    copy = pltpu.make_async_copy(count_vec, count_ref, sem)
    copy.start()

    for fetch in fetches[4:]:
        fetch.wait()
    for b in range(NLB):
        n = min(LB, W - b * LB)
        turn = (TPAD - b * LB) % W
        for plane in range(2):
            rows = fresnel_ref[plane, b * LB : b * LB + n, :].astype(F32)
            block = pltpu.roll(rows, turn, 1)[:, :LK]
            if plane == 0:
                lw_ref[b, 0:n, 0:LK] = block.astype(BF16)
                lw_ref[b, LB : LB + n, LK : 2 * LK] = block.astype(BF16)
            else:
                lw_ref[b, 0:n, LK : 2 * LK] = (-block).astype(BF16)
                lw_ref[b, LB : LB + n, 0:LK] = block.astype(BF16)
    for b, (lo, hi) in enumerate(RIGHT_SPANS):
        k = hi - lo
        real = fresnel_ref[0, b * 128 : (b + 1) * 128, lo:hi]
        imag = fresnel_ref[1, b * 128 : (b + 1) * 128, lo:hi]
        rws[b][0:128, 0:k] = real
        rws[b][0:128, k : 2 * k] = -imag
        rws[b][128:256, 0:k] = imag
        rws[b][128:256, k : 2 * k] = real
    trans0[...] = jnp.zeros_like(trans0)
    trans1[...] = jnp.zeros_like(trans1)

    out_ref[1] = modes_ref[1].astype(F32)
    copy.wait()

    def chunk_range(w, j, t):
        around = [jnp.where(bucket > NG // BUCKET, NCH, 0) for bucket in buckets_of(w, t)]
        starts = []
        most = jnp.int32(0)
        long = jnp.int32(0)
        for l in range(CUTS):
            start, head, end, tail = [
                count_ref[CUTS * j + l, 4 * kind + TILES * w + t] + around[kind] for kind in range(4)
            ]
            most = jnp.maximum(most, jnp.minimum(end - start, NCH))
            short = (start + 1 <= head) & (start + PASS - 1 >= tail)
            long = jnp.maximum(long, jnp.where(short, 0, 1))
            starts.append(start)
        return starts, most, long

    def fill(w, j, t, starts, steps, left, right, spans=None):
        first, wraps = place(w, t)
        shift = corners_ref[w, 0] & (TR - 1)
        rows = jnp.broadcast_to(((iota((TR, 1), 0) + shift) & (TR - 1)).astype(F32), (TR, CH)).astype(BF16)
        step = iota((CT, 1), 0)
        gap = jnp.where(step >= NG - first, GAP, 0)
        columns = jnp.broadcast_to((step - CT // 2 + gap).astype(F32), (CT, CH)).astype(BF16)
        origin = (first + CT // 2).astype(F32)
        beyond = jnp.where(wraps, NG // 2, -1).astype(F32)
        for l in range(CUTS):
            for n, m in enumerate(steps):
                chunk = (starts[l] + m) & (NCH - 1)
                at = pl.ds((CUTS * j + l) * NCH + chunk, 1)
                c = l * len(steps) + n
                fall = fall_ref[at, :]
                column = col_ref[at, :]
                column = column - origin + jnp.where(column < beyond, float(NG + GAP), 0.0)
                column = jnp.clip(column, -CLIP, CLIP)
                column16 = jnp.broadcast_to(column, (16, CH)).astype(BF16)
                fall16 = jnp.broadcast_to(fall, (16, CH)).astype(BF16)
                low, high = spans[n] if spans else (0, CT)
                for s in range(low // 16, high // 16):
                    far = columns[16 * s : 16 * s + 16] - column16
                    right[c, 16 * s : 16 * s + 16, :] = jnp.exp2(far * far * fall16)
                row16 = jnp.broadcast_to(row_ref[at, :], (16, CH)).astype(BF16)
                profile = []
                for s in range(TR // 16):
                    far = rows[16 * s : 16 * s + 16] - row16
                    profile.append(jnp.exp2(far * far * fall16))
                bins = jnp.broadcast_to(bin_ref[at, :], (8, CH))
                strength = jnp.broadcast_to(str_ref[at, :], (8, CH))
                for k in range(SLICES):
                    scale = jnp.where(bins == k, strength, 0.0)
                    scale = jnp.concatenate([scale, scale], axis=0).astype(BF16)
                    for s in range(TR // 16):
                        left[c, k * TR + 16 * s : k * TR + 16 * s + 16, :] = profile[s] * scale

    def product(left, right, chunks=CUTS * PASS):
        wide = [jnp.concatenate([ref[c, 0:CT, :] for c in range(chunks)], axis=1) for ref in (left, right)]
        return nt(*wide)

    def own_rows(w):
        return jnp.broadcast_to(iota((TR, 1), 0) + (corners_ref[w, 0] & (TR - 1)) < TR, (TR, CT))

    def store(w, j, t, value, keep=False):
        own = own_rows(w)
        lanes = pl.ds(t * CT, CT) if isinstance(t, int) else pl.ds(pl.multiple_of(t * CT, CT), CT)
        for k in range(SLICES):
            new = value[k * TR : (k + 1) * TR].astype(BF16)
            pot_ref[w, j, k, :, lanes] = jnp.where(own, pot_ref[w, j, k, :, lanes], new)
            if keep:
                new = jnp.where(own, new, pot_ref[w, j + 1, k, :, lanes])
            pot_ref[w, j + 1, k, :, lanes] = new

    def window_blocks(n, count):
        w, j = which(n)
        values = [product(left, right) for left, right in buffers]
        for t, (left, right) in enumerate(buffers):
            starts, most, long = chunk_range(w, j, t)
            busy_ref[count] = TILES * n + t
            count = count + jnp.where(most > PASS, 1, long)
            fill(w, j, t, starts, range(PASS), left, right, SPANS)
        before = which(jnp.maximum(n - 1, 0))
        for t, value in enumerate(values):
            store(*before, t, value)
        return count

    buffers = ((left0, right0), (left1, right1))
    for _, right in buffers:
        for c in range(CUTS * PASS):
            low, high = SPANS[c % PASS]
            if low > 0:
                right[c, 0:low, :] = jnp.zeros((low, CH), BF16)
            if high < CT:
                right[c, high:CT, :] = jnp.zeros((CT - high, CH), BF16)
    count = lax.fori_loop(0, PB * HALO, window_blocks, jnp.int32(0))
    for t, (left, right) in enumerate(buffers):
        store(PB - 1, HALO - 1, t, product(left, right))

    def crowded(i, carry):
        entry = busy_ref[i]
        w, j = which(entry // TILES)
        t = entry & (TILES - 1)
        starts, most, _ = chunk_range(w, j, t)
        fill(w, j, t, starts, range(PASS), left0, right0)
        acc_ref[...] = product(left0, right0)

        def one_more(m, carry):
            fill(w, j, t, starts, [m], left0, right0)
            acc_ref[...] += product(left0, right0, CUTS)
            return carry

        lax.fori_loop(PASS, jnp.maximum(most, PASS), one_more, 0)
        store(w, j, t, acc_ref[...], keep=True)
        return carry

    lax.fori_loop(0, count, crowded, 0)

    def transmit(w, k, trans, i, waves):
        rows = slice(i * GR, (i + 1) * GR)
        block, part = i * GR // TR, i * GR % TR
        turns = pot_ref[w, block + 1, k, part : part + GR, :].astype(F32) * PHASE
        turns = turns - jnp.round(turns)
        square = turns * turns
        cosine = jnp.full_like(square, COS[-1])
        sine = jnp.full_like(square, SIN[-1])
        for a, b in zip(COS[-2::-1], SIN[-2::-1]):
            cosine = cosine * square + a
            sine = sine * square + b
        sine = sine * turns
        real = waves[w, 0, rows, :].astype(F32)
        imag = waves[w, 1, rows, :].astype(F32)
        into = slice(i * GR + TPAD, (i + 1) * GR + TPAD)
        trans[0, into, :] = (real * cosine - imag * sine).astype(BF16)
        trans[1, into, :] = (real * sine + imag * cosine).astype(BF16)

    def left_product(trans, half, b):
        n = min(LB, W - b * LB)
        rows = slice(b * LB, b * LB + LK)
        both = jnp.concatenate([trans[0, rows, :], trans[1, rows, :]], axis=0)
        product = nn(lw_ref[b], both).astype(BF16)
        half[0, b * LB : b * LB + n, :] = product[0:n]
        half[1, b * LB : b * LB + n, :] = product[LB : LB + n]

    def right_product(w, half, b):
        lo, hi = RIGHT_SPANS[b]
        both = jnp.concatenate([half[0, :, lo:hi], half[1, :, lo:hi]], axis=1)
        product = nt(both, rws[b][...])
        out_ref[w, 0, :, b * 128 : (b + 1) * 128] = product[:, :128]
        out_ref[w, 1, :, b * 128 : (b + 1) * 128] = product[:, 128:]

    def stage(right, left, waves=out_ref, then=None):
        spans = [functools.partial(right_product, *right, b) for b in range(4)] if right else []
        done = 0
        for b in range(NLB):
            if b < len(spans):
                spans[b]()
                if then:
                    then(b)
            if left:
                w, k, trans, half = left
                until = min(W // GR, -(-(b * LB + LK - TPAD) // GR))
                for i in range(done, until):
                    transmit(w, k, trans, i, waves)
                done = until
                left_product(trans, half, b)

    def send(w, b):
        lanes = slice(b * 128, (b + 1) * 128)
        return pltpu.make_async_copy(out_ref.at[w, :, :, lanes], out_hbm.at[w, :, :, lanes], out_sems.at[w, b])

    stage(None, (0, 0, trans0, half0), waves=modes_ref)

    def one_slice(k, carry):
        @pl.when(k < SLICES)
        def _():
            stage((0, half0), (1, k, trans1, half1))

        @pl.when(k < SLICES - 1)
        def _():
            stage((1, half1), (0, k + 1, trans0, half0))

        return carry

    lax.fori_loop(0, SLICES, one_slice, 0)
    for b in range(4):
        send(0, b).start()
    stage((1, half1), None, then=lambda b: send(1, b).start())
    for w in range(PB):
        for b in range(4):
            send(w, b).wait()


def compute(corners, amp, width, lists, modes, fresnel):
    hbm = pl.BlockSpec(memory_space=pltpu.HBM)
    field = pltpu.VMEM((LISTS * NCH, CH), F32)
    return pl.pallas_call(
        compute_kernel,
        out_shape=jax.ShapeDtypeStruct((PB, 2, W, W), F32),
        in_specs=[hbm] * 6,
        out_specs=hbm,
        scratch_shapes=[
            pltpu.SMEM((PB, 2), jnp.int32),
            pltpu.SMEM((NSPEC,), F32),
            pltpu.SMEM((NSPEC,), F32),
            pltpu.VMEM((LISTS, PACK, CH), jnp.int16),
            pltpu.VMEM((PB, 2, W, W), BF16),
            pltpu.VMEM((2, W, W), BF16),
            pltpu.VMEM((PB, 2, W, W), F32),
            field,
            field,
            field,
            field,
            field,
            pltpu.VMEM((LISTS, CH), jnp.int32),
            pltpu.SMEM((LISTS, CH), jnp.int32),
            pltpu.VMEM((CUTS * PASS, SLICES * TR + 16, CH), BF16),
            pltpu.VMEM((CUTS * PASS, CT + 16, CH), BF16),
            pltpu.VMEM((CUTS * PASS, SLICES * TR + 16, CH), BF16),
            pltpu.VMEM((CUTS * PASS, CT + 16, CH), BF16),
            pltpu.VMEM((SLICES * TR, CT), F32),
            pltpu.VMEM((PB, HALO + 1, SLICES, TR, W), BF16),
            pltpu.VMEM((2, TPAD + W + 80, W), BF16),
            pltpu.VMEM((2, TPAD + W + 80, W), BF16),
            pltpu.VMEM((2, W, W), BF16),
            pltpu.VMEM((2, W, W), BF16),
            pltpu.VMEM((NLB, 2 * LB, 2 * LK), BF16),
        ]
        + [pltpu.VMEM((256, 2 * (hi - lo)), BF16) for lo, hi in RIGHT_SPANS]
        + [pltpu.SemaphoreType.DMA, pltpu.SMEM((PB * HALO * 2 + 1,), jnp.int32), pltpu.SemaphoreType.DMA((6,)), pltpu.SemaphoreType.DMA((PB, 4))],
        compiler_params=pltpu.CompilerParams(vmem_limit_bytes=60 * 1024 * 1024),
        name="windows_and_slices",
    )(corners, amp, width, lists, modes, fresnel)


def gather_lists(cells, bins, species):
    vmem = pl.BlockSpec(memory_space=pltpu.VMEM)
    passed = HALO * 2
    return pl.pallas_call(
        lists_kernel,
        out_shape=jax.ShapeDtypeStruct((LISTS, PACK, CH), jnp.int16),
        in_specs=[vmem, vmem, vmem],
        out_specs=pl.BlockSpec(memory_space=pltpu.HBM),
        scratch_shapes=[
            pltpu.VMEM((PACK, CH), jnp.int16),
            pltpu.SemaphoreType.DMA,
            pltpu.SemaphoreType.DMA((passed,)),
            pltpu.SemaphoreType.DMA((passed,)),
            pltpu.SemaphoreType.DMA((LISTS,)),
        ],
        compiler_params=pltpu.CompilerParams(collective_id=0, has_side_effects=True),
        name="sort_and_gather",
    )(cells, bins, species)


def body(
    probe_modes,
    probe_corners,
    atom_cells,
    atom_bins,
    atom_species,
    species_amp,
    species_width,
    fresnel,
):
    lists = gather_lists(atom_cells.T, atom_bins.T, atom_species.reshape(1, -1))
    return compute(probe_corners, species_amp, species_width, lists, probe_modes, fresnel)


def solution(mesh):
    return jax.shard_map(
        body,
        mesh=mesh,
        in_specs=(
            P(("cuts", "probe"), None, None, None),
            P(("cuts", "probe"), None),
            P(("cuts", "probe"), None),
            P(("cuts", "probe"), None),
            P(("cuts", "probe")),
            P(),
            P(),
            P(),
        ),
        out_specs=P(("cuts", "probe"), None, None, None),
        check_vma=False,
    )
```

```python
import functools

import jax
import jax.numpy as jnp
from jax import lax
from jax.experimental import pallas as pl
from jax.experimental.pallas import tpu as pltpu
from jax.sharding import PartitionSpec as P

NG = 2048
W = 512
TR = 64
NSPEC = 4
NA = 2048
SLICES = 4
CUTS = 4
PROBE = 32
PB = 2

HALO = 9
LISTS = HALO * CUTS
CH = 128
NCH = NA // CH
BUCKET = 16
FIELDS = 4
PACK = FIELDS * NCH
TILES = 2
UNPACK = 12
REACH = 13.7
CT = 256
GAP = 32
CLIP = 224.0
PASS = 4
HEAD = 176
TAIL = 128
SPANS = ((0, HEAD), (0, CT), (0, CT), (TAIL, CT))
MESH = pl.DeviceIdType.MESH
F32 = jnp.float32
BF16 = jnp.bfloat16

PHASE = 0.4 / 6.283185307179586
COS = (
    0.9999590208378119,
    -19.73094236686191,
    64.67144177616537,
    -82.390806311774,
    45.62105110286101,
)
SIN = (
    6.2831611294861265,
    -41.3368318308275,
    81.44770647022538,
    -74.90941970419655,
    33.548355145172366,
)


def nn(a, b):
    return lax.dot_general(a, b, (((1,), (0,)), ((), ())), preferred_element_type=F32)


def nt(a, b):
    return lax.dot_general(a, b, (((1,), (1,)), ((), ())), preferred_element_type=F32)


def iota(shape, dim):
    return lax.broadcasted_iota(jnp.int32, shape, dim)


def sort_into(cells_ref, bins_ref, species_ref, out_ref):
    before = (iota((CH, CH), 0) < iota((CH, CH), 1)).astype(F32).astype(BF16)
    below = (iota((CH, CH), 1) < iota((CH, CH), 0)).astype(F32).astype(BF16)
    ones = jnp.ones((CH, CH), BF16)
    buckets = iota((CH, CH), 0)
    chunks = [slice(c * CH, (c + 1) * CH) for c in range(NCH)]
    hots = [(buckets == cells_ref[1:2, lanes] // BUCKET).astype(F32) for lanes in chunks]
    tall = jnp.concatenate([hot.astype(BF16) for hot in hots], axis=0)
    sums = nn(tall, jnp.concatenate([before, ones], axis=1))
    running = jnp.zeros((CH, CH), F32)
    prefixes = []
    for lanes in chunks:
        prefixes.append(sums[lanes, :CH] + running)
        running = running + sums[lanes, CH:]
    high = jnp.floor(running * (1.0 / 64.0))
    low = running - 64.0 * high
    offset = 64.0 * nn(below, high.astype(BF16)) + nn(below, low.astype(BF16))
    lefts = []
    rights = []
    for lanes, hot, prefix in zip(chunks, hots, prefixes):
        rank = jnp.sum(hot * (prefix + offset), axis=0, keepdims=True).astype(jnp.int32)
        row = cells_ref[0:1, lanes] & (TR - 1)
        column = cells_ref[1:2, lanes]
        fields = (row, column // 64, column & 63, species_ref[0:1, lanes], bins_ref[0:1, lanes])
        chosen = (iota((NCH, CH), 0) == rank // CH).astype(F32)
        lefts.append(jnp.concatenate([chosen * f.astype(F32) for f in fields], axis=0).astype(BF16))
        rights.append((buckets == (rank & (CH - 1))).astype(F32).astype(BF16))
    sorted_fields = nt(jnp.concatenate(lefts, axis=1), jnp.concatenate(rights, axis=1))
    row, high, low, kind, bins = [sorted_fields[f * NCH : (f + 1) * NCH] for f in range(5)]
    for f, field in enumerate((row, 64.0 * high + low, kind, bins)):
        out_ref[f * NCH : (f + 1) * NCH, :] = field.astype(jnp.int32).astype(jnp.int16)


def lists_kernel(cells_ref, bins_ref, species_ref, out_ref, own_ref, local_sem, send_sems, pass_sems, recv_sems):
    g = lax.axis_index("cuts")
    q = lax.axis_index("probe")
    core = lax.rem(g, 2)
    sibling = (g + 1 - 2 * core, q)
    barrier = pltpu.get_barrier_semaphore()
    pairs = [(j, r) for j in (1, 2, 0, 3, 4, 5, 6, 7, 8) for r in (0, 2) if (j, r) != (1, 0)]

    def holder(j, r):
        return lax.rem(g + r, CUTS), lax.rem(q + j - 1 + PROBE, PROBE)

    def reader(j, r):
        return lax.rem(g + r, CUTS), lax.rem(q + 1 - j + PROBE, PROBE)

    def remote(src, slot, send_sem, device):
        return pltpu.make_async_remote_copy(
            src_ref=src,
            dst_ref=out_ref.at[slot],
            send_sem=send_sem,
            recv_sem=recv_sems.at[slot],
            device_id=device,
            device_id_type=MESH,
        )

    pl.semaphore_signal(barrier, inc=1, device_id=sibling, device_id_type=MESH)
    for j, r in pairs:
        pl.semaphore_signal(barrier, inc=1, device_id=holder(j, r), device_id_type=MESH)
    sort_into(cells_ref, bins_ref, species_ref, own_ref)
    local = pltpu.make_async_copy(own_ref, out_ref.at[CUTS + g], local_sem)
    local.start()
    pl.semaphore_wait(barrier, len(pairs) + 1)
    sends = []
    for n, (j, r) in enumerate(pairs):
        sends.append(remote(own_ref, CUTS * j + g, send_sems.at[n], reader(j, r)))
    sends.append(remote(own_ref, CUTS + g, pass_sems.at[len(pairs)], sibling))
    for copy in sends:
        copy.start()
    for n, (j, r) in enumerate(pairs):
        slot = CUTS * j + lax.rem(g + r, CUTS)
        remote(own_ref, slot, send_sems.at[n], sibling).wait_recv()
        onward = remote(out_ref.at[slot], slot, pass_sems.at[n], sibling)
        onward.start()
        sends.append(onward)
    for j in range(HALO):
        for r in (1, 3):
            slot = CUTS * j + lax.rem(g + r, CUTS)
            remote(own_ref, slot, send_sems.at[0], sibling).wait_recv()
    for copy in sends:
        copy.wait_send()
    local.wait()


GR = 16
LB = 96
LK = 128
NLB = -(-W // LB)
TPAD = 16
RIGHT_SPANS = ((0, 256), (0, 384), (128, 512), (256, 512))


def compute_kernel(
    corners_hbm,
    amp_hbm,
    width_hbm,
    lists_hbm,
    modes_hbm,
    fresnel_hbm,
    out_hbm,
    corners_ref,
    amp_ref,
    width_ref,
    lists_ref,
    modes_ref,
    fresnel_ref,
    out_ref,
    col_ref,
    fall_ref,
    row_ref,
    str_ref,
    bin_ref,
    count_vec,
    count_ref,
    left0,
    right0,
    left1,
    right1,
    acc_ref,
    pot_ref,
    trans0,
    trans1,
    half0,
    half1,
    lw_ref,
    rw0,
    rw1,
    rw2,
    rw3,
    sem,
    busy_ref,
    in_sems,
    out_sems,
):
    rws = (rw0, rw1, rw2, rw3)
    sources = (lists_hbm, corners_hbm, amp_hbm, width_hbm, fresnel_hbm, modes_hbm)
    targets = (lists_ref, corners_ref, amp_ref, width_ref, fresnel_ref, modes_ref)
    fetches = [pltpu.make_async_copy(a, b, in_sems.at[n]) for n, (a, b) in enumerate(zip(sources, targets))]
    for fetch in fetches:
        fetch.start()
    for fetch in fetches[:4]:
        fetch.wait()

    widest = width_ref[0]
    for species in range(1, NSPEC):
        widest = jnp.maximum(widest, width_ref[species])
    reach = (widest * REACH).astype(jnp.int32) + 1

    def which(n):
        w = jnp.where(n >= HALO, 1, 0)
        return w, n - HALO * w

    def place(w, t):
        first = (corners_ref[w, 1] + t * CT) & (NG - 1)
        return first, first + CT > NG

    def buckets_of(w, t):
        first, wraps = place(w, t)
        most = jnp.where(wraps, 2 * NG, NG) // BUCKET
        last = first + CT - 1 + reach
        return (
            jnp.maximum(first - reach, 0) // BUCKET,
            (first + HEAD - reach) // BUCKET,
            jnp.minimum(last // BUCKET + 1, most),
            jnp.minimum((first + TAIL + reach + BUCKET - 1) // BUCKET, most),
        )

    lane = iota((1, CH), 1)
    edge = jnp.zeros((1, CH), jnp.int32)
    for n in range(PB * TILES):
        for kind, bucket in enumerate(buckets_of(n // TILES, n % TILES)):
            bucket = jnp.where(bucket > NG // BUCKET, bucket - NG // BUCKET, bucket)
            edge = jnp.where(lane == 4 * kind + n, bucket * BUCKET, edge)
    edge = jnp.broadcast_to(edge.astype(F32), (NCH, CH))
    by_tail = iota((NCH, CH), 1) < 8

    def unpack_list(i):
        def part(f):
            return lists_ref[i, f * NCH : (f + 1) * NCH, :].astype(jnp.int32)

        species = part(2)
        amp = jnp.zeros((NCH, CH), F32)
        width = jnp.zeros((NCH, CH), F32)
        for s in range(NSPEC):
            amp = jnp.where(species == s, amp_ref[s], amp)
            width = jnp.where(species == s, width_ref[s], width)
        column = part(1).astype(F32)
        rows = pl.ds(pl.multiple_of(i * NCH, NCH), NCH)
        row_ref[rows, :] = part(0).astype(F32)
        col_ref[rows, :] = column
        fall_ref[rows, :] = -0.7213475204444817 / (width * width)
        str_ref[rows, :] = amp
        bin_ref[rows, :] = part(3).astype(F32)
        tail = jnp.broadcast_to(column[:, CH - 1 : CH], (NCH, CH))
        head = jnp.broadcast_to(column[:, 0:1], (NCH, CH))
        below = (jnp.where(by_tail, tail, head) < edge).astype(F32)
        count_vec[pl.ds(i, 1), :] = jnp.sum(below, axis=0, keepdims=True).astype(jnp.int32)

    def unpack(n, carry):
        for l in range(UNPACK):
            unpack_list(UNPACK * n + l)
        return carry

    lax.fori_loop(0, LISTS // UNPACK, unpack, 0)
    copy = pltpu.make_async_copy(count_vec, count_ref, sem)
    copy.start()

    for fetch in fetches[4:]:
        fetch.wait()
    for b in range(NLB):
        n = min(LB, W - b * LB)
        turn = (TPAD - b * LB) % W
        for plane in range(2):
            rows = fresnel_ref[plane, b * LB : b * LB + n, :].astype(F32)
            block = pltpu.roll(rows, turn, 1)[:, :LK]
            if plane == 0:
                lw_ref[b, 0:n, 0:LK] = block.astype(BF16)
                lw_ref[b, LB : LB + n, LK : 2 * LK] = block.astype(BF16)
            else:
                lw_ref[b, 0:n, LK : 2 * LK] = (-block).astype(BF16)
                lw_ref[b, LB : LB + n, 0:LK] = block.astype(BF16)
    for b, (lo, hi) in enumerate(RIGHT_SPANS):
        k = hi - lo
        real = fresnel_ref[0, b * 128 : (b + 1) * 128, lo:hi]
        imag = fresnel_ref[1, b * 128 : (b + 1) * 128, lo:hi]
        rws[b][0:128, 0:k] = real
        rws[b][0:128, k : 2 * k] = -imag
        rws[b][128:256, 0:k] = imag
        rws[b][128:256, k : 2 * k] = real
    for trans in (trans0, trans1):
        trans[:, 0:TPAD, :] = jnp.zeros((2, TPAD, W), BF16)
        trans[:, TPAD + W : TPAD + W + 80, :] = jnp.zeros((2, 80, W), BF16)

    out_ref[1] = modes_ref[1].astype(F32)
    copy.wait()

    def chunk_range(w, j, t):
        around = [jnp.where(bucket > NG // BUCKET, NCH, 0) for bucket in buckets_of(w, t)]
        starts = []
        most = jnp.int32(0)
        long = jnp.int32(0)
        for l in range(CUTS):
            start, head, end, tail = [
                count_ref[CUTS * j + l, 4 * kind + TILES * w + t] + around[kind] for kind in range(4)
            ]
            most = jnp.maximum(most, jnp.minimum(end - start, NCH))
            short = (start + 1 <= head) & (start + PASS - 1 >= tail)
            long = jnp.maximum(long, jnp.where(short, 0, 1))
            starts.append(start)
        return starts, most, long

    def fill(w, j, t, starts, steps, left, right, spans=None):
        first, wraps = place(w, t)
        shift = corners_ref[w, 0] & (TR - 1)
        rows = jnp.broadcast_to(((iota((TR, 1), 0) + shift) & (TR - 1)).astype(F32), (TR, CH)).astype(BF16)
        step = iota((CT, 1), 0)
        gap = jnp.where(step >= NG - first, GAP, 0)
        columns = jnp.broadcast_to((step - CT // 2 + gap).astype(F32), (CT, CH)).astype(BF16)
        origin = (first + CT // 2).astype(F32)
        beyond = jnp.where(wraps, NG // 2, -1).astype(F32)
        for l in range(CUTS):
            for n, m in enumerate(steps):
                chunk = (starts[l] + m) & (NCH - 1)
                at = pl.ds((CUTS * j + l) * NCH + chunk, 1)
                c = l * len(steps) + n
                fall = fall_ref[at, :]
                column = col_ref[at, :]
                column = column - origin + jnp.where(column < beyond, float(NG + GAP), 0.0)
                column = jnp.clip(column, -CLIP, CLIP)
                column16 = jnp.broadcast_to(column, (16, CH)).astype(BF16)
                fall16 = jnp.broadcast_to(fall, (16, CH)).astype(BF16)
                low, high = spans[n] if spans else (0, CT)
                for s in range(low // 16, high // 16):
                    far = columns[16 * s : 16 * s + 16] - column16
                    right[c, 16 * s : 16 * s + 16, :] = jnp.exp2(far * far * fall16)
                row16 = jnp.broadcast_to(row_ref[at, :], (16, CH)).astype(BF16)
                profile = []
                for s in range(TR // 16):
                    far = rows[16 * s : 16 * s + 16] - row16
                    profile.append(jnp.exp2(far * far * fall16))
                bins = jnp.broadcast_to(bin_ref[at, :], (8, CH))
                strength = jnp.broadcast_to(str_ref[at, :], (8, CH))
                for k in range(SLICES):
                    scale = jnp.where(bins == k, strength, 0.0)
                    scale = jnp.concatenate([scale, scale], axis=0).astype(BF16)
                    for s in range(TR // 16):
                        left[c, k * TR + 16 * s : k * TR + 16 * s + 16, :] = profile[s] * scale

    def product(left, right, chunks=CUTS * PASS):
        wide = [jnp.concatenate([ref[c, 0:CT, :] for c in range(chunks)], axis=1) for ref in (left, right)]
        return nt(*wide)

    def own_rows(w):
        return jnp.broadcast_to(iota((TR, 1), 0) + (corners_ref[w, 0] & (TR - 1)) < TR, (TR, CT))

    def store(w, j, t, value, keep=False):
        own = own_rows(w)
        lanes = pl.ds(t * CT, CT) if isinstance(t, int) else pl.ds(pl.multiple_of(t * CT, CT), CT)
        for k in range(SLICES):
            new = value[k * TR : (k + 1) * TR].astype(BF16)
            pot_ref[w, j, k, :, lanes] = jnp.where(own, pot_ref[w, j, k, :, lanes], new)
            if keep:
                new = jnp.where(own, new, pot_ref[w, j + 1, k, :, lanes])
            pot_ref[w, j + 1, k, :, lanes] = new

    def window_blocks(n, count):
        w, j = which(n)
        values = [product(left, right) for left, right in buffers]
        for t, (left, right) in enumerate(buffers):
            starts, most, long = chunk_range(w, j, t)
            busy_ref[count] = TILES * n + t
            count = count + jnp.where(most > PASS, 1, long)
            fill(w, j, t, starts, range(PASS), left, right, SPANS)
        before = which(jnp.maximum(n - 1, 0))
        for t, value in enumerate(values):
            store(*before, t, value)
        return count

    buffers = ((left0, right0), (left1, right1))
    for _, right in buffers:
        for c in range(CUTS * PASS):
            low, high = SPANS[c % PASS]
            if low > 0:
                right[c, 0:low, :] = jnp.zeros((low, CH), BF16)
            if high < CT:
                right[c, high:CT, :] = jnp.zeros((CT - high, CH), BF16)
    count = lax.fori_loop(0, PB * HALO, window_blocks, jnp.int32(0))
    for t, (left, right) in enumerate(buffers):
        store(PB - 1, HALO - 1, t, product(left, right))

    def crowded(i, carry):
        entry = busy_ref[i]
        w, j = which(entry // TILES)
        t = entry & (TILES - 1)
        starts, most, _ = chunk_range(w, j, t)
        fill(w, j, t, starts, range(PASS), left0, right0)
        acc_ref[...] = product(left0, right0)

        def one_more(m, carry):
            fill(w, j, t, starts, [m], left0, right0)
            acc_ref[...] += product(left0, right0, CUTS)
            return carry

        lax.fori_loop(PASS, jnp.maximum(most, PASS), one_more, 0)
        store(w, j, t, acc_ref[...], keep=True)
        return carry

    lax.fori_loop(0, count, crowded, 0)

    def transmit(w, k, trans, i, waves):
        rows = slice(i * GR, (i + 1) * GR)
        block, part = i * GR // TR, i * GR % TR
        turns = pot_ref[w, block + 1, k, part : part + GR, :].astype(F32) * PHASE
        turns = turns - jnp.round(turns)
        square = turns * turns
        cosine = jnp.full_like(square, COS[-1])
        sine = jnp.full_like(square, SIN[-1])
        for a, b in zip(COS[-2::-1], SIN[-2::-1]):
            cosine = cosine * square + a
            sine = sine * square + b
        sine = sine * turns
        real = waves[w, 0, rows, :].astype(F32)
        imag = waves[w, 1, rows, :].astype(F32)
        into = slice(i * GR + TPAD, (i + 1) * GR + TPAD)
        trans[0, into, :] = (real * cosine - imag * sine).astype(BF16)
        trans[1, into, :] = (real * sine + imag * cosine).astype(BF16)

    def left_product(trans, half, b):
        n = min(LB, W - b * LB)
        rows = slice(b * LB, b * LB + LK)
        both = jnp.concatenate([trans[0, rows, :], trans[1, rows, :]], axis=0)
        product = nn(lw_ref[b], both).astype(BF16)
        half[0, b * LB : b * LB + n, :] = product[0:n]
        half[1, b * LB : b * LB + n, :] = product[LB : LB + n]

    def right_product(w, half, b):
        lo, hi = RIGHT_SPANS[b]
        both = jnp.concatenate([half[0, :, lo:hi], half[1, :, lo:hi]], axis=1)
        product = nt(both, rws[b][...])
        out_ref[w, 0, :, b * 128 : (b + 1) * 128] = product[:, :128]
        out_ref[w, 1, :, b * 128 : (b + 1) * 128] = product[:, 128:]

    def stage(right, left, waves=out_ref, then=None):
        spans = [functools.partial(right_product, *right, b) for b in range(4)] if right else []
        done = 0
        for b in range(NLB):
            if b < len(spans):
                spans[b]()
                if then:
                    then(b)
            if left:
                w, k, trans, half = left
                until = min(W // GR, -(-(b * LB + LK - TPAD) // GR))
                for i in range(done, until):
                    transmit(w, k, trans, i, waves)
                done = until
                left_product(trans, half, b)

    def send(w, b):
        lanes = slice(b * 128, (b + 1) * 128)
        return pltpu.make_async_copy(out_ref.at[w, :, :, lanes], out_hbm.at[w, :, :, lanes], out_sems.at[w, b])

    stage(None, (0, 0, trans0, half0), waves=modes_ref)

    def one_slice(k, carry):
        @pl.when(k < SLICES)
        def _():
            stage((0, half0), (1, k, trans1, half1))

        @pl.when(k < SLICES - 1)
        def _():
            stage((1, half1), (0, k + 1, trans0, half0))

        return carry

    lax.fori_loop(0, SLICES, one_slice, 0)
    for b in range(4):
        send(0, b).start()
    stage((1, half1), None, then=lambda b: send(1, b).start())
    for w in range(PB):
        for b in range(4):
            send(w, b).wait()


def compute(corners, amp, width, lists, modes, fresnel):
    hbm = pl.BlockSpec(memory_space=pltpu.HBM)
    field = pltpu.VMEM((LISTS * NCH, CH), F32)
    return pl.pallas_call(
        compute_kernel,
        out_shape=jax.ShapeDtypeStruct((PB, 2, W, W), F32),
        in_specs=[hbm] * 6,
        out_specs=hbm,
        scratch_shapes=[
            pltpu.SMEM((PB, 2), jnp.int32),
            pltpu.SMEM((NSPEC,), F32),
            pltpu.SMEM((NSPEC,), F32),
            pltpu.VMEM((LISTS, PACK, CH), jnp.int16),
            pltpu.VMEM((PB, 2, W, W), BF16),
            pltpu.VMEM((2, W, W), BF16),
            pltpu.VMEM((PB, 2, W, W), F32),
            field,
            field,
            field,
            field,
            field,
            pltpu.VMEM((LISTS, CH), jnp.int32),
            pltpu.SMEM((LISTS, CH), jnp.int32),
            pltpu.VMEM((CUTS * PASS, SLICES * TR + 16, CH), BF16),
            pltpu.VMEM((CUTS * PASS, CT + 16, CH), BF16),
            pltpu.VMEM((CUTS * PASS, SLICES * TR + 16, CH), BF16),
            pltpu.VMEM((CUTS * PASS, CT + 16, CH), BF16),
            pltpu.VMEM((SLICES * TR, CT), F32),
            pltpu.VMEM((PB, HALO + 1, SLICES, TR, W), BF16),
            pltpu.VMEM((2, TPAD + W + 80, W), BF16),
            pltpu.VMEM((2, TPAD + W + 80, W), BF16),
            pltpu.VMEM((2, W, W), BF16),
            pltpu.VMEM((2, W, W), BF16),
            pltpu.VMEM((NLB, 2 * LB, 2 * LK), BF16),
        ]
        + [pltpu.VMEM((256, 2 * (hi - lo)), BF16) for lo, hi in RIGHT_SPANS]
        + [pltpu.SemaphoreType.DMA, pltpu.SMEM((PB * HALO * 2 + 1,), jnp.int32), pltpu.SemaphoreType.DMA((6,)), pltpu.SemaphoreType.DMA((PB, 4))],
        compiler_params=pltpu.CompilerParams(vmem_limit_bytes=60 * 1024 * 1024),
        name="windows_and_slices",
    )(corners, amp, width, lists, modes, fresnel)


def gather_lists(cells, bins, species):
    vmem = pl.BlockSpec(memory_space=pltpu.VMEM)
    passed = HALO * 2
    return pl.pallas_call(
        lists_kernel,
        out_shape=jax.ShapeDtypeStruct((LISTS, PACK, CH), jnp.int16),
        in_specs=[vmem, vmem, vmem],
        out_specs=pl.BlockSpec(memory_space=pltpu.HBM),
        scratch_shapes=[
            pltpu.VMEM((PACK, CH), jnp.int16),
            pltpu.SemaphoreType.DMA,
            pltpu.SemaphoreType.DMA((passed,)),
            pltpu.SemaphoreType.DMA((passed,)),
            pltpu.SemaphoreType.DMA((LISTS,)),
        ],
        compiler_params=pltpu.CompilerParams(collective_id=0, has_side_effects=True),
        name="sort_and_gather",
    )(cells, bins, species)


def body(
    probe_modes,
    probe_corners,
    atom_cells,
    atom_bins,
    atom_species,
    species_amp,
    species_width,
    fresnel,
):
    lists = gather_lists(atom_cells.T, atom_bins.T, atom_species.reshape(1, -1))
    return compute(probe_corners, species_amp, species_width, lists, probe_modes, fresnel)


def solution(mesh):
    return jax.shard_map(
        body,
        mesh=mesh,
        in_specs=(
            P(("cuts", "probe"), None, None, None),
            P(("cuts", "probe"), None),
            P(("cuts", "probe"), None),
            P(("cuts", "probe"), None),
            P(("cuts", "probe")),
            P(),
            P(),
            P(),
        ),
        out_specs=P(("cuts", "probe"), None, None, None),
        check_vma=False,
    )
```
